256 devices in a mesh: section: 8 (over y, core), expert: 32 (over z, x).
Axes of the slice: x: 4, y: 4, z: 8, core: 2. Of those that a mesh axis runs over, the one named last changes fastest.
Arguments:
- tokens: bfloat16 [4096, 7168], P('expert', 'section'), may hold values from -6 to 6
- routes: int32 [4096, 8], P('expert'), may hold values from 0 to 63, all different within a row; in each aligned block of 128 rows (0 to 127, 128 to 255, ...) at most 24 rows name the same one
- combine: float32 [4096, 8], P('expert'), may hold values from 0.05 to 0.6
- gate_weight: bfloat16 [64, 7168, 1024], P('expert', 'section'), may hold values from -0.0625 to 0.0625
- up_weight: bfloat16 [64, 7168, 1024], P('expert', 'section'), may hold values from -0.0625 to 0.0625
- down_weight: bfloat16 [64, 1024, 7168], P('expert', None, 'section'), may hold values from -0.1875 to 0.1875
Outputs:
- mixed: bfloat16 [4096, 7168], P('expert', 'section')
The draws below stay inside these ranges and needn't reach their ends.
Inputs may be any that keep to these rules, and one draw needn't show every extreme that they name: `routes`: among the 128 rows of one block of tokens, no expert is named more than 24 times; in every draw some expert is named exactly 24 times in some block. The 8 experts of a token differ.
All inputs are finite; a program needn't handle non-finite values.
Results may differ from the reference program's by a relative error of at most 0.029.
Values may be sent and summed in bfloat16 or wider, within the bound.
No kernel may reach another device: no remote copies, remote signals or barrier semaphores. Data moves between devices by JAX's collectives and lax.ppermute only.
A program may use at most 64 MiB of HBM per device.

```python
import math
import jax
import jax.numpy as jnp
import numpy as np
from jax import lax

D = 7168
FF = 1024
TOP = 8
TOK_DEV = 128
EXPERTS = 64
TOKENS = 4096
CAP = 24
N_SECTION = 8
N_EXPERT = 32


def block_levels(rng, extent, split, smallest, high):
    def one(axis_at, shards_of):
        heights = jax.random.uniform(jax.random.fold_in(jax.random.fold_in(rng, 6), axis_at), (shards_of,), jnp.float32, smallest / len(split), high / len(split))
        return jnp.repeat(jnp.exp(heights), extent[axis_at] // shards_of).reshape((-1,) + (1,) * (len(extent) - axis_at - 1))

    gain = one(*split[0])
    for cut in split[1:]:
        gain = gain * one(*cut)
    return gain


def deal_out(stream_key, own, number, rows, amount, top, most, skew):
    ranking = jax.random.permutation(stream_key, amount)
    heavy_load, usual = shares(amount, rows * top, most, skew, True), shares(amount, rows * top, most, skew, False)
    places = jnp.arange(amount)

    def named(lengths, offset_by):
        used = int((lengths > 0).sum())
        fixed = max(1, used // 4)
        shifted = fixed + (places - fixed + offset_by * (used - fixed)) % max(1, amount - fixed)
        return jnp.zeros((amount,), jnp.int32).at[ranking[jnp.where(places < fixed, places, shifted)]].set(jnp.asarray(lengths, jnp.int32))

    lengths = jnp.where(number % 4 == 0, named(heavy_load, number // 4), named(usual, number - number // 4 - 1))
    mixed = jax.random.permutation(jax.random.fold_in(own, 3), amount)
    donor, sink = mixed[0:amount // 2 * 2:2], mixed[1:amount // 2 * 2:2]
    room = jnp.minimum(lengths[donor] - 1, most - lengths[sink]) // 2
    room = jnp.where((donor == ranking[0]) | (sink == ranking[0]) | (lengths[sink] == 0), 0, jnp.maximum(room, 0))
    shifted = jax.random.randint(jax.random.fold_in(own, 4), (amount // 2,), 0, 1 << 20) % (room + 1)
    lengths = lengths.at[donor].add(-shifted).at[sink].add(shifted)
    items = jnp.searchsorted(jnp.cumsum(lengths), jnp.arange(rows * top), side="right").astype(jnp.int32)
    listing = items.reshape(top, rows).T
    listing = listing[jax.random.permutation(jax.random.fold_in(own, 1), rows)]
    offset_by = jax.random.randint(jax.random.fold_in(own, 2), (rows, 1), 0, top)
    return jnp.take_along_axis(listing, (jnp.arange(top)[None, :] + offset_by) % top, axis=1)


def shares(count, total, reach, lean, full):
    weights = [(1 << 20) // math.isqrt(grade ** lean) + 1 for grade in range(1, count + 1)]
    largest = reach if full else min(reach, max(-(-total // count), total * weights[0] // sum(weights)))
    least = 1 if total - largest >= count - 1 else 0
    holding, rest = [largest] + [least] * (count - 1), total - largest - least * (count - 1)
    while rest > 0:
        movable = [i for i in range(1, count) if holding[i] < largest] or [i for i in range(1, count) if holding[i] < reach]
        pool, left = sum([weights[i] for i in movable]), rest
        for i in movable:
            addition = min(reach - holding[i], max(1, left * weights[i] // pool), rest)
            holding[i] = holding[i] + addition
            rest = rest - addition
    return np.array(holding)


def noise(stream_key, extent, deviation, most, cuts=(), kind=jnp.bfloat16):
    gain = block_levels(stream_key, extent, cuts, -0.22, 0.18) if cuts else 1.0
    result = jax.random.normal(stream_key, extent, jnp.float32) * deviation * gain
    return jnp.minimum(jnp.maximum(result, -most), most).astype(kind)


def setup_inputs(seed: int = 0) -> dict:
    key_of = jax.random.split(jax.random.key(seed), 7)
    tokens = noise(key_of[0], (TOKENS, D), 1.0, 6.0, ((0, 32), (1, 8)))
    routes_keys = jax.random.split(jax.random.fold_in(key_of[1], 1), TOKENS // TOK_DEV)
    routes_turns = jax.random.permutation(jax.random.fold_in(key_of[1], 3), TOKENS // TOK_DEV)
    routes = jax.vmap(lambda own, number: deal_out(jax.random.fold_in(key_of[1], 2), own, number, TOK_DEV, EXPERTS, TOP, CAP, 2))(routes_keys, routes_turns).reshape((TOKENS, TOP))
    combine = jnp.clip(0.05 + 0.55 * jax.random.uniform(key_of[2], (TOKENS, TOP), jnp.float32) ** block_levels(key_of[2], (TOKENS, TOP), ((0, 32),), -0.2, 0.2), 0.05, 0.6)
    gate_weight = noise(key_of[3], (EXPERTS, D, FF), D ** -0.5, 0.0625, ((0, 32), (1, 8)))
    up_weight = noise(key_of[4], (EXPERTS, D, FF), D ** -0.5, 0.0625, ((0, 32), (1, 8)))
    down_weight = noise(key_of[5], (EXPERTS, FF, D), FF ** -0.5, 0.1875, ((0, 32), (2, 8)))
    return dict(tokens=tokens, routes=routes, combine=combine, gate_weight=gate_weight, up_weight=up_weight, down_weight=down_weight)


def slot_positions(routes):
    route_blocks = routes.reshape(N_EXPERT, TOK_DEV * TOP)
    onehot = (route_blocks[:, :, None] == jnp.arange(EXPERTS, dtype=jnp.int32)[None, None, :]).astype(jnp.int32)
    ranks = jnp.cumsum(onehot, axis=1) * onehot
    return route_blocks, (jnp.sum(ranks, axis=2) - 1).astype(jnp.int32)


def rounded_sum(terms):
    narrow = lax.optimization_barrier(terms.astype(jnp.bfloat16))
    return jnp.sum(narrow.astype(jnp.float32), axis=0)


def expert_rows(operands):
    slab_rows, gate_w, up_w, down_w = operands
    part_width = D // N_SECTION
    pieces = slab_rows.astype(jnp.float32).reshape(slab_rows.shape[0], N_SECTION, part_width)
    gate_terms = jnp.einsum("rsd,sdf->srf", pieces, gate_w.astype(jnp.float32).reshape(N_SECTION, part_width, FF))
    up_terms = jnp.einsum("rsd,sdf->srf", pieces, up_w.astype(jnp.float32).reshape(N_SECTION, part_width, FF))
    gate = rounded_sum(gate_terms)
    up_sum = rounded_sum(up_terms)
    hidden = (jax.nn.silu(gate) * up_sum).astype(jnp.bfloat16)
    return jnp.dot(hidden, down_w, preferred_element_type=jnp.float32).astype(jnp.bfloat16)


def reference(tokens, routes, combine, gate_weight, up_weight, down_weight):
    route_blocks, slot_index = slot_positions(routes)
    source_dev = jnp.broadcast_to(jnp.arange(N_EXPERT, dtype=jnp.int32)[:, None], route_blocks.shape)
    owner_row = jnp.arange(TOK_DEV * TOP, dtype=jnp.int32) // TOP
    token_blocks = tokens.reshape(N_EXPERT, TOK_DEV, D)
    picked = token_blocks[source_dev, owner_row[None, :]]
    buffer = jnp.zeros((EXPERTS, N_EXPERT, CAP, D), jnp.bfloat16)
    buffer = buffer.at[route_blocks, source_dev, slot_index].set(picked)
    outputs = lax.map(expert_rows, (buffer.reshape(EXPERTS, N_EXPERT * CAP, D), gate_weight, up_weight, down_weight))
    outputs = outputs.reshape(EXPERTS, N_EXPERT, CAP, D)
    returned = outputs[route_blocks, source_dev, slot_index].astype(jnp.float32)
    returned = returned.reshape(N_EXPERT, TOK_DEV, TOP, D)
    weights = combine.reshape(N_EXPERT, TOK_DEV, TOP, 1)
    mixed = jnp.sum(returned * weights, axis=2)
    return mixed.reshape(TOKENS, D).astype(jnp.bfloat16)
```

```python
import functools

import jax
import jax.numpy as jnp
from jax import lax
from jax.experimental import pallas as pl
from jax.experimental.pallas import tpu as pltpu
from jax.sharding import PartitionSpec as P

BF16, F32 = jnp.bfloat16, jnp.float32
NX, CORES = 4, 2
CHUNKS = ((1, -1), (2, -2), (3, -3), (0, 4))
VMEM = pl.BlockSpec(memory_space=pltpu.VMEM)
SMEM = pl.BlockSpec(memory_space=pltpu.SMEM)


def along_expert(value, dz, dx):
    count = lax.axis_size("expert")
    planes = count // NX
    return lax.ppermute(
        value,
        "expert",
        [(i, (i // NX + dz) % planes * NX + (i % NX + dx) % NX) for i in range(count)],
    )


def along_section(value, dy, flip):
    count = lax.axis_size("section")
    return lax.ppermute(
        value, "section", [(i, (i + CORES * dy) % count ^ flip) for i in range(count)]
    )


def call(kernel, outs, specs=None, grid=(), out_specs=None, scratch=(), limit=12, flops=0, moved=0):
    return pl.pallas_call(
        kernel,
        grid=grid,
        out_shape=outs,
        in_specs=specs,
        out_specs=out_specs or jax.tree.map(lambda _: VMEM, outs),
        scratch_shapes=scratch,
        compiler_params=pltpu.CompilerParams(vmem_limit_bytes=limit << 20),
        cost_estimate=pl.CostEstimate(flops=flops, bytes_accessed=moved, transcendentals=0),
    )


def select_kernel(capacity, rows, at_ref, *refs):
    nz = len(refs) - 6
    blocks, outs, code_ref, weight_ref = refs[:nz], refs[nz : nz + 4], refs[-2], refs[-1]
    per_plane = 2 * NX
    row = lax.broadcasted_iota(jnp.int32, (per_plane, rows), 0)
    expert = (at_ref[0] * per_plane + (at_ref[1] + row // 2) % NX * 2 + row % 2).astype(F32)
    earlier = (
        lax.broadcasted_iota(jnp.int32, (rows, rows), 0)
        < lax.broadcasted_iota(jnp.int32, (rows, rows), 1)
    ).astype(F32).astype(BF16)
    codes = []
    for n, block in enumerate(blocks):
        info = block[pl.ds(rows, 16), pl.ds(0, rows)].astype(F32)
        named = jnp.zeros((per_plane, rows), F32)
        weight = jnp.zeros((per_plane, rows), F32)
        for k in range(8):
            hit = info[k : k + 1] == expert
            named = named + jnp.where(hit, 1.0, 0.0)
            weight = weight + jnp.where(hit, info[8 + k : 9 + k], 0.0)
        slot = jnp.dot(named.astype(BF16), earlier, preferred_element_type=F32)
        codes.append(jnp.where(named > 0.5, slot + float(n * capacity), -1.0))
        weight_ref[:, pl.ds(n * rows, rows)] = weight
    code = jnp.concatenate(codes, axis=1)
    code_ref[...] = code
    held = nz * capacity
    at = lax.broadcasted_iota(jnp.int32, (held, nz * rows), 0).astype(F32)
    tokens = jnp.concatenate([block[pl.ds(0, rows), :] for block in blocks], axis=0)
    for r in range(NX):
        pick = jnp.concatenate(
            [jnp.where(at == code[2 * r + e : 2 * r + e + 1], 1.0, 0.0) for e in range(2)], axis=0
        ).astype(BF16)
        outs[r][...] = jnp.dot(pick, tokens, preferred_element_type=F32).astype(BF16)


def up_kernel(held, at_ref, *refs):
    rows, gate_ref, up_ref, keep_ref, send_ref, x_ref = refs[:4], *refs[4:]
    core, y = at_ref[3], at_ref[2]

    @pl.when(pl.program_id(0) == 0)
    def _():
        for r in range(4):
            for e in range(2):
                x_ref[e, pl.ds(r * held, held), :] = rows[r][pl.ds(e * held, held), :]

    for out_ref, e in ((keep_ref, core), (send_ref, 1 - core)):
        x = x_ref[e]
        for part, weight_ref in enumerate((gate_ref, up_ref)):
            sums = jnp.dot(x, weight_ref[e], preferred_element_type=F32).astype(BF16)
            for r in range(4):
                out_ref[(r + 4 - y) % 4, part] = sums[r * held : (r + 1) * held]


def join_kernel(keep_ref, got_ref, *outs):
    for q in range(4):
        outs[q][...] = (keep_ref[q].astype(F32) + got_ref[q].astype(F32)).astype(BF16)


def silu_kernel(a_ref, b_ref, c_ref, d_ref, out_ref):
    gate, up = (
        (a_ref[i].astype(F32) + b_ref[i].astype(F32)) + (c_ref[i].astype(F32) + d_ref[i].astype(F32))
        for i in range(2)
    )
    out_ref[...] = (jax.nn.silu(gate) * up).astype(BF16)


def down_kernel(held, at_ref, *refs):
    parts, down_ref, outs, h_ref = refs[:8], refs[8], refs[9:13], refs[13]
    core, y = at_ref[3], at_ref[2]

    @pl.when(pl.program_id(0) == 0)
    def _():
        for q in range(4):
            for f in range(2):
                at = pl.multiple_of((y + 4 - q) % 4 * held, held)
                h_ref[(core + f) % 2, pl.ds(at, held), :] = parts[2 * q + f][...]

    got = jnp.dot(h_ref[pl.program_id(0)], down_ref[0], preferred_element_type=F32).astype(BF16)
    for r in range(4):
        outs[r][...] = got[r * held : (r + 1) * held]


def mix_kernel(held, rows, a_ref, b_ref, c_ref, d_ref, code_ref, weight_ref, *outs):
    width = code_ref.shape[1]
    at = lax.broadcasted_iota(jnp.int32, (held, width), 0).astype(F32)
    share = jnp.concatenate(
        [
            jnp.where(at == code_ref[j : j + 1, :], weight_ref[j : j + 1, :], 0.0)
            for j in range(2 * NX)
        ],
        axis=0,
    ).astype(BF16)
    back = jnp.concatenate([ref[...] for ref in (a_ref, b_ref, c_ref, d_ref)], axis=0)
    total = lax.dot_general(
        share, back, (((0,), (0,)), ((), ())), preferred_element_type=F32
    ).astype(BF16)
    for n, out in enumerate(outs):
        out[...] = total[n * rows : (n + 1) * rows]


def shape(*dims, dtype=BF16):
    return jax.ShapeDtypeStruct(dims, dtype)


def body(tokens, routes, combine, gate_weight, up_weight, down_weight):
    groups = lax.axis_size("expert")
    per_device, width, units = gate_weight.shape
    rows, fanout = routes.shape
    capacity = 3 * rows * fanout // (2 * per_device * groups)
    place, part = lax.axis_index("expert"), lax.axis_index("section")
    at = jnp.stack([place // NX, place % NX, part // CORES, part % CORES]).astype(jnp.int32)

    info = jnp.concatenate([routes.T.astype(BF16), combine.T.astype(BF16)], axis=0)
    message = jnp.concatenate([tokens, jnp.pad(info, ((0, 0), (0, width - rows)))], axis=0)

    partials = []
    for chunk in CHUNKS:
        nz = len(chunk)
        held = nz * capacity
        blocks = [along_expert(message, d, 0) if d else message for d in chunk]
        *picked, code, weight = call(
            functools.partial(select_kernel, capacity, rows),
            [shape(2 * held, width)] * 4 + [shape(2 * NX, nz * rows, dtype=F32)] * 2,
            [SMEM] + [VMEM] * nz,
            flops=16 * held * nz * rows * width,
            moved=2 << 20,
        )(at, *blocks)
        came = [along_expert(picked[r], 0, r) if r else picked[r] for r in range(4)]
        tile = 256
        whole = lambda i: (0, 0)
        keep, send = call(
            functools.partial(up_kernel, held),
            [shape(4, 2, held, units)] * 2,
            [SMEM]
            + [pl.BlockSpec((2 * held, width), whole)] * 4
            + [pl.BlockSpec((2, width, tile), lambda i: (0, 0, i))] * 2,
            grid=(units // tile,),
            out_specs=[pl.BlockSpec((4, 2, held, tile), lambda i: (0, 0, 0, i))] * 2,
            scratch=[pltpu.VMEM((2, 4 * held, width), BF16)],
            flops=32 * held * width * units,
            moved=10 << 20,
        )(at, *came, gate_weight, up_weight)
        got = along_section(send, 0, 1)
        sums = call(
            join_kernel, [shape(2, held, units)] * 4, [VMEM] * 2, moved=3 << 20
        )(keep, got)
        terms = [along_section(sums[q], q, 0) if q else sums[q] for q in range(4)]
        hidden = call(silu_kernel, shape(held, units), [VMEM] * 4, moved=1 << 20)(*terms)
        parts = [
            along_section(hidden, q, f) if q or f else hidden for q in range(4) for f in range(2)
        ]
        out = call(
            functools.partial(down_kernel, held),
            [shape(2 * held, width)] * 4,
            [SMEM]
            + [pl.BlockSpec((held, units), whole)] * 8
            + [pl.BlockSpec((1, units, width), lambda i: (i, 0, 0))],
            grid=(2,),
            out_specs=[pl.BlockSpec((held, width), lambda i: (i, 0))] * 4,
            scratch=[pltpu.VMEM((2, 4 * held, units), BF16)],
            flops=16 * held * width * units,
            moved=6 << 20,
        )(at, *parts, down_weight)
        back = [along_expert(out[r], 0, -r) if r else out[r] for r in range(4)]
        mixed = call(
            functools.partial(mix_kernel, held, rows),
            [shape(rows, width)] * nz,
            [VMEM] * 6,
            flops=16 * held * nz * rows * width,
            moved=2 << 20,
        )(*back, code, weight)
        partials += [along_expert(m, -d, 0) if d else m for d, m in zip(chunk, mixed)]
    return sum(p.astype(F32) for p in partials).astype(BF16)


def solution(mesh):
    return jax.shard_map(
        body,
        mesh=mesh,
        in_specs=(
            P("expert", "section"),
            P("expert", None),
            P("expert", None),
            P("expert", "section", None),
            P("expert", "section", None),
            P("expert", None, "section"),
        ),
        out_specs=P("expert", "section"),
        check_vma=False,
    )
```

```python
import functools

import jax
import jax.numpy as jnp
from jax import lax
from jax.experimental import pallas as pl
from jax.experimental.pallas import tpu as pltpu
from jax.sharding import PartitionSpec as P

BF16, F32 = jnp.bfloat16, jnp.float32
NX, CORES = 4, 2
CHUNKS = ((1, -1, 2, -2), (0, 4, 3, -3))
VMEM = pl.BlockSpec(memory_space=pltpu.VMEM)
SMEM = pl.BlockSpec(memory_space=pltpu.SMEM)


def along_expert(value, dz, dx):
    count = lax.axis_size("expert")
    planes = count // NX
    return lax.ppermute(
        value,
        "expert",
        [(i, (i // NX + dz) % planes * NX + (i % NX + dx) % NX) for i in range(count)],
    )


def along_section(value, dy, flip):
    count = lax.axis_size("section")
    return lax.ppermute(
        value, "section", [(i, (i + CORES * dy) % count ^ flip) for i in range(count)]
    )


def call(kernel, outs, specs=None, grid=(), out_specs=None, scratch=(), limit=24, flops=0, moved=0):
    return pl.pallas_call(
        kernel,
        grid=grid,
        out_shape=outs,
        in_specs=specs,
        out_specs=out_specs or jax.tree.map(lambda _: VMEM, outs),
        scratch_shapes=scratch,
        compiler_params=pltpu.CompilerParams(vmem_limit_bytes=limit << 20),
        cost_estimate=pl.CostEstimate(flops=flops, bytes_accessed=moved, transcendentals=0),
    )


def select_kernel(capacity, rows, at_ref, *refs):
    nz = len(refs) - 6
    blocks, outs, code_ref, weight_ref = refs[:nz], refs[nz : nz + 4], refs[-2], refs[-1]
    per_plane = 2 * NX
    row = lax.broadcasted_iota(jnp.int32, (per_plane, rows), 0)
    expert = (at_ref[0] * per_plane + (at_ref[1] + row // 2) % NX * 2 + row % 2).astype(F32)
    earlier = (
        lax.broadcasted_iota(jnp.int32, (rows, rows), 0)
        < lax.broadcasted_iota(jnp.int32, (rows, rows), 1)
    ).astype(F32).astype(BF16)
    codes = []
    for n, block in enumerate(blocks):
        info = block[pl.ds(rows, 16), pl.ds(0, rows)].astype(F32)
        named = jnp.zeros((per_plane, rows), F32)
        weight = jnp.zeros((per_plane, rows), F32)
        for k in range(8):
            hit = info[k : k + 1] == expert
            named = named + jnp.where(hit, 1.0, 0.0)
            weight = weight + jnp.where(hit, info[8 + k : 9 + k], 0.0)
        slot = jnp.dot(named.astype(BF16), earlier, preferred_element_type=F32)
        codes.append(jnp.where(named > 0.5, slot + float(n * capacity), -1.0))
        weight_ref[:, pl.ds(n * rows, rows)] = weight
    code = jnp.concatenate(codes, axis=1)
    code_ref[...] = code
    held = nz * capacity
    at = lax.broadcasted_iota(jnp.int32, (held, nz * rows), 0).astype(F32)
    tokens = jnp.concatenate([block[pl.ds(0, rows), :] for block in blocks], axis=0)
    for r in range(NX):
        pick = jnp.concatenate(
            [jnp.where(at == code[2 * r + e : 2 * r + e + 1], 1.0, 0.0) for e in range(2)], axis=0
        ).astype(BF16)
        outs[r][...] = jnp.dot(pick, tokens, preferred_element_type=F32).astype(BF16)


def up_kernel(held, at_ref, *refs):
    rows, gate_ref, up_ref, keep_ref, send_ref, x_ref = refs[:4], *refs[4:]
    core, y = at_ref[3], at_ref[2]

    @pl.when(pl.program_id(0) == 0)
    def _():
        for r in range(4):
            for e in range(2):
                x_ref[e, pl.ds(r * held, held), :] = rows[r][pl.ds(e * held, held), :]

    for out_ref, e in ((keep_ref, core), (send_ref, 1 - core)):
        x = x_ref[e]
        for part, weight_ref in enumerate((gate_ref, up_ref)):
            sums = jnp.dot(x, weight_ref[e], preferred_element_type=F32).astype(BF16)
            for r in range(4):
                out_ref[(r + 4 - y) % 4, part] = sums[r * held : (r + 1) * held]


def join_kernel(keep_ref, got_ref, *outs):
    for q in range(4):
        outs[q][...] = (keep_ref[q].astype(F32) + got_ref[q].astype(F32)).astype(BF16)


def silu_kernel(a_ref, b_ref, c_ref, d_ref, out_ref):
    gate, up = (
        (a_ref[i].astype(F32) + b_ref[i].astype(F32)) + (c_ref[i].astype(F32) + d_ref[i].astype(F32))
        for i in range(2)
    )
    out_ref[...] = (jax.nn.silu(gate) * up).astype(BF16)


def down_kernel(held, at_ref, *refs):
    parts, down_ref, outs, h_ref = refs[:2], refs[2], refs[3:7], refs[7]
    core, y = at_ref[3], at_ref[2]

    @pl.when(pl.program_id(0) == 0)
    def _():
        for q in range(4):
            for f in range(2):
                at = pl.multiple_of((y + 4 - q) % 4 * held, held)
                h_ref[(core + f) % 2, pl.ds(at, held), :] = parts[f][q]

    got = jnp.dot(h_ref[pl.program_id(0)], down_ref[0], preferred_element_type=F32).astype(BF16)
    for r in range(4):
        outs[r][...] = got[r * held : (r + 1) * held]


def mix_kernel(held, rows, a_ref, b_ref, c_ref, d_ref, code_ref, weight_ref, *outs):
    width = code_ref.shape[1]
    at = lax.broadcasted_iota(jnp.int32, (held, width), 0).astype(F32)
    share = jnp.concatenate(
        [
            jnp.where(at == code_ref[j : j + 1, :], weight_ref[j : j + 1, :], 0.0)
            for j in range(2 * NX)
        ],
        axis=0,
    ).astype(BF16)
    back = jnp.concatenate([ref[...] for ref in (a_ref, b_ref, c_ref, d_ref)], axis=0)
    total = lax.dot_general(
        share, back, (((0,), (0,)), ((), ())), preferred_element_type=F32
    ).astype(BF16)
    for n, out in enumerate(outs):
        out[...] = total[n * rows : (n + 1) * rows]


def shape(*dims, dtype=BF16):
    return jax.ShapeDtypeStruct(dims, dtype)


def body(tokens, routes, combine, gate_weight, up_weight, down_weight):
    groups = lax.axis_size("expert")
    per_device, width, units = gate_weight.shape
    rows, fanout = routes.shape
    capacity = 3 * rows * fanout // (2 * per_device * groups)
    place, part = lax.axis_index("expert"), lax.axis_index("section")
    at = jnp.stack([place // NX, place % NX, part // CORES, part % CORES]).astype(jnp.int32)

    info = jnp.concatenate([routes.T.astype(BF16), combine.T.astype(BF16)], axis=0)
    message = jnp.concatenate([tokens, jnp.pad(info, ((0, 0), (0, width - rows)))], axis=0)

    partials = []
    blocks = ()
    for chunk in CHUNKS:
        nz = len(chunk)
        held = nz * capacity
        sent, _ = lax.optimization_barrier((message, blocks))
        blocks = [along_expert(sent, d, 0) if d else sent for d in chunk]
        *picked, code, weight = call(
            functools.partial(select_kernel, capacity, rows),
            [shape(2 * held, width)] * 4 + [shape(2 * NX, nz * rows, dtype=F32)] * 2,
            [SMEM] + [VMEM] * nz,
            flops=16 * held * nz * rows * width,
            moved=2 << 20,
        )(at, *blocks)
        came = [along_expert(picked[r], 0, r) if r else picked[r] for r in range(4)]
        tile = 256
        whole = lambda i: (0, 0)
        keep, send = call(
            functools.partial(up_kernel, held),
            [shape(4, 2, held, units)] * 2,
            [SMEM]
            + [pl.BlockSpec((2 * held, width), whole)] * 4
            + [pl.BlockSpec((2, width, tile), lambda i: (0, 0, i))] * 2,
            grid=(units // tile,),
            out_specs=[pl.BlockSpec((4, 2, held, tile), lambda i: (0, 0, 0, i))] * 2,
            scratch=[pltpu.VMEM((2, 4 * held, width), BF16)],
            flops=32 * held * width * units,
            moved=10 << 20,
        )(at, *came, gate_weight, up_weight)
        got = along_section(send, 0, 1)
        sums = call(
            join_kernel, [shape(2, held, units)] * 4, [VMEM] * 2, moved=3 << 20
        )(keep, got)
        terms = [along_section(sums[q], q, 0) if q else sums[q] for q in range(4)]
        hidden = call(silu_kernel, shape(held, units), [VMEM] * 4, moved=1 << 20)(*terms)
        parts = jnp.stack([along_section(hidden, q, 0) if q else hidden for q in range(4)])
        others = along_section(parts, 0, 1)
        out = call(
            functools.partial(down_kernel, held),
            [shape(2 * held, width)] * 4,
            [SMEM]
            + [pl.BlockSpec((4, held, units), lambda i: (0, 0, 0))] * 2
            + [pl.BlockSpec((1, units, width), lambda i: (i, 0, 0))],
            grid=(2,),
            out_specs=[pl.BlockSpec((held, width), lambda i: (i, 0))] * 4,
            scratch=[pltpu.VMEM((2, 4 * held, units), BF16)],
            flops=16 * held * width * units,
            moved=6 << 20,
        )(at, parts, others, down_weight)
        back = [along_expert(out[r], 0, -r) if r else out[r] for r in range(4)]
        mixed = call(
            functools.partial(mix_kernel, held, rows),
            [shape(rows, width)] * nz,
            [VMEM] * 6,
            flops=16 * held * nz * rows * width,
            moved=2 << 20,
        )(*back, code, weight)
        partials += [along_expert(m, -d, 0) if d else m for d, m in zip(chunk, mixed)]
    return sum(p.astype(F32) for p in partials).astype(BF16)


def solution(mesh):
    return jax.shard_map(
        body,
        mesh=mesh,
        in_specs=(
            P("expert", "section"),
            P("expert", None),
            P("expert", None),
            P("expert", "section", None),
            P("expert", "section", None),
            P("expert", None, "section"),
        ),
        out_specs=P("expert", "section"),
        check_vma=False,
    )
```

```python
import functools

import jax
import jax.numpy as jnp
from jax import lax
from jax.experimental import pallas as pl
from jax.experimental.pallas import tpu as pltpu
from jax.sharding import PartitionSpec as P

BF16, F32 = jnp.bfloat16, jnp.float32
NX, CORES = 4, 2
CHUNKS = ((1, -1), (2, -2), (3, -3), (0, 4))
VMEM = pl.BlockSpec(memory_space=pltpu.VMEM)
SMEM = pl.BlockSpec(memory_space=pltpu.SMEM)


def along_expert(value, dz, dx):
    count = lax.axis_size("expert")
    planes = count // NX
    return lax.ppermute(
        value,
        "expert",
        [(i, (i // NX + dz) % planes * NX + (i % NX + dx) % NX) for i in range(count)],
    )


def along_section(value, dy, flip):
    count = lax.axis_size("section")
    return lax.ppermute(
        value, "section", [(i, (i + CORES * dy) % count ^ flip) for i in range(count)]
    )


def call(kernel, outs, specs=None, grid=(), out_specs=None, scratch=(), limit=16, flops=0, moved=0):
    return pl.pallas_call(
        kernel,
        grid=grid,
        out_shape=outs,
        in_specs=specs,
        out_specs=out_specs or jax.tree.map(lambda _: VMEM, outs),
        scratch_shapes=scratch,
        compiler_params=pltpu.CompilerParams(vmem_limit_bytes=limit << 20),
        cost_estimate=pl.CostEstimate(flops=flops, bytes_accessed=moved, transcendentals=0),
    )


def select_kernel(capacity, rows, at_ref, *refs):
    nz = len(refs) - 3
    blocks, (out_ref, code_ref, weight_ref) = refs[:nz], refs[nz:]
    per_plane = 2 * NX
    row = lax.broadcasted_iota(jnp.int32, (per_plane, rows), 0)
    expert = (at_ref[0] * per_plane + row).astype(F32)
    earlier = (
        lax.broadcasted_iota(jnp.int32, (rows, rows), 0)
        < lax.broadcasted_iota(jnp.int32, (rows, rows), 1)
    ).astype(F32).astype(BF16)
    codes = []
    for n, block in enumerate(blocks):
        info = block[pl.ds(rows, 16), pl.ds(0, rows)].astype(F32)
        named = jnp.zeros((per_plane, rows), F32)
        weight = jnp.zeros((per_plane, rows), F32)
        for k in range(8):
            hit = info[k : k + 1] == expert
            named = named + jnp.where(hit, 1.0, 0.0)
            weight = weight + jnp.where(hit, info[8 + k : 9 + k], 0.0)
        slot = jnp.dot(named.astype(BF16), earlier, preferred_element_type=F32)
        codes.append(jnp.where(named > 0.5, slot + float(n * capacity), -1.0))
        weight_ref[:, pl.ds(n * rows, rows)] = weight
    code = jnp.concatenate(codes, axis=1)
    code_ref[...] = code
    held = nz * capacity
    at = lax.broadcasted_iota(jnp.int32, (held, nz * rows), 0).astype(F32)
    tokens = jnp.concatenate([block[pl.ds(0, rows), :] for block in blocks], axis=0)
    for r in range(NX):
        pick = jnp.concatenate(
            [jnp.where(at == code[2 * r + e : 2 * r + e + 1], 1.0, 0.0) for e in range(2)], axis=0
        ).astype(BF16)
        out_ref[r] = jnp.dot(pick, tokens, preferred_element_type=F32).astype(BF16)


def up_kernel(held, at_ref, rows_ref, gate_ref, up_ref, keep_ref, send_ref, x_ref):
    core = at_ref[1]

    @pl.when(pl.program_id(0) == 0)
    def _():
        for r in range(4):
            for e in range(2):
                x_ref[e, pl.ds(r * held, held), :] = rows_ref[r, pl.ds(e * held, held), :]

    for out_ref, e in ((keep_ref, core), (send_ref, 1 - core)):
        x = x_ref[e]
        for part, weight_ref in enumerate((gate_ref, up_ref)):
            sums = jnp.dot(x, weight_ref[e], preferred_element_type=F32).astype(BF16)
            for r in range(4):
                out_ref[r, part] = sums[r * held : (r + 1) * held]


def join_kernel(keep_ref, got_ref, out_ref):
    out_ref[...] = (keep_ref[...].astype(F32) + got_ref[...].astype(F32)).astype(BF16)


def silu_kernel(terms_ref, out_ref):
    gate, up = (
        (terms_ref[0, i].astype(F32) + terms_ref[1, i].astype(F32))
        + (terms_ref[2, i].astype(F32) + terms_ref[3, i].astype(F32))
        for i in range(2)
    )
    hidden = (jax.nn.silu(gate) * up).astype(BF16)
    for q in range(4):
        out_ref[q] = hidden


def down_kernel(held, at_ref, own_ref, other_ref, down_ref, out_ref):
    core = at_ref[1]
    for parts_ref, e in ((own_ref, core), (other_ref, 1 - core)):
        hidden = parts_ref[...].reshape(4 * held, parts_ref.shape[2])
        got = jnp.dot(hidden, down_ref[e], preferred_element_type=F32).astype(BF16)
        for r in range(4):
            out_ref[r, e] = got[r * held : (r + 1) * held]


def mix_kernel(held, rows, back_ref, code_ref, weight_ref, *outs):
    width = code_ref.shape[1]
    at = lax.broadcasted_iota(jnp.int32, (held, width), 0).astype(F32)
    share = jnp.concatenate(
        [
            jnp.where(at == code_ref[j : j + 1, :], weight_ref[j : j + 1, :], 0.0)
            for j in range(2 * NX)
        ],
        axis=0,
    ).astype(BF16)
    total = lax.dot_general(
        share,
        back_ref[...].reshape(share.shape[0], back_ref.shape[3]),
        (((0,), (0,)), ((), ())),
        preferred_element_type=F32,
    ).astype(BF16)
    for n, out in enumerate(outs):
        out[...] = total[n * rows : (n + 1) * rows]


def shape(*dims, dtype=BF16):
    return jax.ShapeDtypeStruct(dims, dtype)


def body(tokens, routes, combine, gate_weight, up_weight, down_weight):
    groups = lax.axis_size("expert")
    per_device, width, units = gate_weight.shape
    rows, fanout = routes.shape
    capacity = 3 * rows * fanout // (2 * per_device * groups)
    place, part = lax.axis_index("expert"), lax.axis_index("section")
    at = jnp.stack([place // NX, part % CORES]).astype(jnp.int32)
    planes = groups // NX
    x_groups = [[z * NX + x for x in range(NX)] for z in range(planes)]
    sections = lax.axis_size("section")
    y_groups = [[y * CORES + c for y in range(sections // CORES)] for c in range(CORES)]

    def swap_x(value):
        return lax.all_to_all(value, "expert", 0, 0, axis_index_groups=x_groups, tiled=True)

    def swap_y(value):
        return lax.all_to_all(value, "section", 0, 0, axis_index_groups=y_groups, tiled=True)

    info = jnp.concatenate([routes.T.astype(BF16), combine.T.astype(BF16)], axis=0)
    block = {0: jnp.concatenate([tokens, jnp.pad(info, ((0, 0), (0, width - rows)))], axis=0)}
    for d in (1, -1, 2, -2, 3, -3, 4):
        step = 1 if d > 0 else -1
        block[d] = along_expert(block[d - step], step, 0)

    partials = []
    for chunk in CHUNKS:
        nz = len(chunk)
        held = nz * capacity
        picked, code, weight = call(
            functools.partial(select_kernel, capacity, rows),
            [shape(4, 2 * held, width)] + [shape(2 * NX, nz * rows, dtype=F32)] * 2,
            [SMEM] + [VMEM] * nz,
            flops=16 * held * nz * rows * width,
            moved=2 << 20,
        )(at, *[block[d] for d in chunk])
        came = swap_x(picked)
        tile = 256
        keep, send = call(
            functools.partial(up_kernel, held),
            [shape(4, 2, held, units)] * 2,
            [SMEM, pl.BlockSpec((4, 2 * held, width), lambda i: (0, 0, 0))]
            + [pl.BlockSpec((2, width, tile), lambda i: (0, 0, i))] * 2,
            grid=(units // tile,),
            out_specs=[pl.BlockSpec((4, 2, held, tile), lambda i: (0, 0, 0, i))] * 2,
            scratch=[pltpu.VMEM((2, 4 * held, width), BF16)],
            flops=32 * held * width * units,
            moved=10 << 20,
        )(at, came, gate_weight, up_weight)
        got = along_section(send, 0, 1)
        sums = call(join_kernel, shape(4, 2, held, units), [VMEM] * 2, moved=3 << 20)(keep, got)
        terms = swap_y(sums)
        hidden = call(silu_kernel, shape(4, held, units), [VMEM], moved=1 << 20)(terms)
        parts = swap_y(hidden)
        others = along_section(parts, 0, 1)
        out = call(
            functools.partial(down_kernel, held),
            shape(4, 2, held, width),
            [SMEM, VMEM, VMEM, VMEM],
            flops=16 * held * width * units,
            moved=6 << 20,
        )(at, parts, others, down_weight)
        back = swap_x(out)
        mixed = call(
            functools.partial(mix_kernel, held, rows),
            [shape(rows, width)] * nz,
            [VMEM] * 3,
            flops=16 * held * nz * rows * width,
            moved=2 << 20,
        )(back, code, weight)
        partials += [along_expert(m, -d, 0) if d else m for d, m in zip(chunk, mixed)]
    return sum(p.astype(F32) for p in partials).astype(BF16)


def solution(mesh):
    return jax.shard_map(
        body,
        mesh=mesh,
        in_specs=(
            P("expert", "section"),
            P("expert", None),
            P("expert", None),
            P("expert", "section", None),
            P("expert", "section", None),
            P("expert", None, "section"),
        ),
        out_specs=P("expert", "section"),
        check_vma=False,
    )
```

```python
import functools

import jax
import jax.numpy as jnp
from jax import lax
from jax.experimental import pallas as pl
from jax.experimental.pallas import tpu as pltpu
from jax.sharding import PartitionSpec as P

BF16, F32 = jnp.bfloat16, jnp.float32
NX, CORES = 4, 2
CHUNKS = ((1, -1, 2, -2), (0, 4, 3, -3))
VMEM = pl.BlockSpec(memory_space=pltpu.VMEM)
SMEM = pl.BlockSpec(memory_space=pltpu.SMEM)


def along_expert(value, dz, dx):
    count = lax.axis_size("expert")
    planes = count // NX
    return lax.ppermute(
        value,
        "expert",
        [(i, (i // NX + dz) % planes * NX + (i % NX + dx) % NX) for i in range(count)],
    )


def along_section(value, dy, flip):
    count = lax.axis_size("section")
    return lax.ppermute(
        value, "section", [(i, (i + CORES * dy) % count ^ flip) for i in range(count)]
    )


def call(kernel, outs, specs=None, grid=(), out_specs=None, scratch=(), limit=20, flops=0, moved=0):
    return pl.pallas_call(
        kernel,
        grid=grid,
        out_shape=outs,
        in_specs=specs,
        out_specs=out_specs or jax.tree.map(lambda _: VMEM, outs),
        scratch_shapes=scratch,
        compiler_params=pltpu.CompilerParams(vmem_limit_bytes=limit << 20),
        cost_estimate=pl.CostEstimate(flops=flops, bytes_accessed=moved, transcendentals=0),
    )


def select_kernel(capacity, rows, at_ref, *refs):
    nz = len(refs) - 3
    blocks, (out_ref, code_ref, weight_ref) = refs[:nz], refs[nz:]
    per_plane = 2 * NX
    row = lax.broadcasted_iota(jnp.int32, (per_plane, rows), 0)
    expert = (at_ref[0] * per_plane + row).astype(F32)
    earlier = (
        lax.broadcasted_iota(jnp.int32, (rows, rows), 0)
        < lax.broadcasted_iota(jnp.int32, (rows, rows), 1)
    ).astype(F32).astype(BF16)
    codes = []
    for n, block in enumerate(blocks):
        info = block[pl.ds(rows, 16), pl.ds(0, rows)].astype(F32)
        named = jnp.zeros((per_plane, rows), F32)
        weight = jnp.zeros((per_plane, rows), F32)
        for k in range(8):
            hit = info[k : k + 1] == expert
            named = named + jnp.where(hit, 1.0, 0.0)
            weight = weight + jnp.where(hit, info[8 + k : 9 + k], 0.0)
        slot = jnp.dot(named.astype(BF16), earlier, preferred_element_type=F32)
        codes.append(jnp.where(named > 0.5, slot + float(n * capacity), -1.0))
        weight_ref[:, pl.ds(n * rows, rows)] = weight
    code = jnp.concatenate(codes, axis=1)
    code_ref[...] = code
    held = nz * capacity
    at = lax.broadcasted_iota(jnp.int32, (held, nz * rows), 0).astype(F32)
    tokens = jnp.concatenate([block[pl.ds(0, rows), :] for block in blocks], axis=0)
    for r in range(NX):
        pick = jnp.concatenate(
            [jnp.where(at == code[2 * r + e : 2 * r + e + 1], 1.0, 0.0) for e in range(2)], axis=0
        ).astype(BF16)
        out_ref[r] = jnp.dot(pick, tokens, preferred_element_type=F32).astype(BF16)


def up_kernel(held, at_ref, rows_ref, gate_ref, up_ref, keep_ref, send_ref, x_ref):
    core = at_ref[1]

    @pl.when(pl.program_id(0) == 0)
    def _():
        for r in range(4):
            for e in range(2):
                x_ref[e, pl.ds(r * held, held), :] = rows_ref[r, pl.ds(e * held, held), :]

    for out_ref, e in ((keep_ref, core), (send_ref, 1 - core)):
        x = x_ref[e]
        for part, weight_ref in enumerate((gate_ref, up_ref)):
            sums = jnp.dot(x, weight_ref[e], preferred_element_type=F32).astype(BF16)
            for r in range(4):
                out_ref[r, part] = sums[r * held : (r + 1) * held]


def join_kernel(keep_ref, got_ref, out_ref):
    out_ref[...] = (keep_ref[...].astype(F32) + got_ref[...].astype(F32)).astype(BF16)


def silu_kernel(terms_ref, out_ref):
    gate, up = (
        (terms_ref[0, i].astype(F32) + terms_ref[1, i].astype(F32))
        + (terms_ref[2, i].astype(F32) + terms_ref[3, i].astype(F32))
        for i in range(2)
    )
    hidden = (jax.nn.silu(gate) * up).astype(BF16)
    for q in range(4):
        out_ref[q] = hidden


def down_kernel(held, at_ref, own_ref, other_ref, down_ref, out_ref, h_ref):
    core = at_ref[1]

    @pl.when(pl.program_id(0) == 0)
    def _():
        h_ref[core] = own_ref[...].reshape(4 * held, own_ref.shape[2])
        h_ref[1 - core] = other_ref[...].reshape(4 * held, own_ref.shape[2])

    hidden = h_ref[pl.program_id(0)]
    got = jnp.dot(hidden, down_ref[0], preferred_element_type=F32).astype(BF16)
    for r in range(4):
        out_ref[r, 0] = got[r * held : (r + 1) * held]


def mix_kernel(held, rows, back_ref, code_ref, weight_ref, *outs):
    width = code_ref.shape[1]
    at = lax.broadcasted_iota(jnp.int32, (held, width), 0).astype(F32)
    share = jnp.concatenate(
        [
            jnp.where(at == code_ref[j : j + 1, :], weight_ref[j : j + 1, :], 0.0)
            for j in range(2 * NX)
        ],
        axis=0,
    ).astype(BF16)
    total = lax.dot_general(
        share,
        back_ref[...].reshape(share.shape[0], back_ref.shape[3]),
        (((0,), (0,)), ((), ())),
        preferred_element_type=F32,
    ).astype(BF16)
    for n, out in enumerate(outs):
        out[...] = total[n * rows : (n + 1) * rows]


def shape(*dims, dtype=BF16):
    return jax.ShapeDtypeStruct(dims, dtype)


def body(tokens, routes, combine, gate_weight, up_weight, down_weight):
    groups = lax.axis_size("expert")
    per_device, width, units = gate_weight.shape
    rows, fanout = routes.shape
    capacity = 3 * rows * fanout // (2 * per_device * groups)
    place, part = lax.axis_index("expert"), lax.axis_index("section")
    at = jnp.stack([place // NX, part % CORES]).astype(jnp.int32)
    planes = groups // NX
    x_groups = [[z * NX + x for x in range(NX)] for z in range(planes)]
    sections = lax.axis_size("section")
    y_groups = [[y * CORES + c for y in range(sections // CORES)] for c in range(CORES)]

    def swap_x(value):
        return lax.all_to_all(value, "expert", 0, 0, axis_index_groups=x_groups, tiled=True)

    def swap_y(value):
        return lax.all_to_all(value, "section", 0, 0, axis_index_groups=y_groups, tiled=True)

    gate_weight, up_weight, down_weight = (
        pltpu.with_memory_space_constraint(w, pltpu.HBM)
        for w in (gate_weight, up_weight, down_weight)
    )
    info = jnp.concatenate([routes.T.astype(BF16), combine.T.astype(BF16)], axis=0)
    block = {0: jnp.concatenate([tokens, jnp.pad(info, ((0, 0), (0, width - rows)))], axis=0)}
    for d in (1, -1, 2, -2, 3, -3, 4):
        step = 1 if d > 0 else -1
        block[d] = along_expert(block[d - step], step, 0)

    partials = []
    for chunk in CHUNKS:
        nz = len(chunk)
        held = nz * capacity
        picked, code, weight = call(
            functools.partial(select_kernel, capacity, rows),
            [shape(4, 2 * held, width)] + [shape(2 * NX, nz * rows, dtype=F32)] * 2,
            [SMEM] + [VMEM] * nz,
            flops=16 * held * nz * rows * width,
            moved=2 << 20,
        )(at, *[block[d] for d in chunk])
        came = swap_x(picked)
        tile = 256
        keep, send = call(
            functools.partial(up_kernel, held),
            [shape(4, 2, held, units)] * 2,
            [SMEM, pl.BlockSpec((4, 2 * held, width), lambda i: (0, 0, 0))]
            + [pl.BlockSpec((2, width, tile), lambda i: (0, 0, i))] * 2,
            grid=(units // tile,),
            out_specs=[pl.BlockSpec((4, 2, held, tile), lambda i: (0, 0, 0, i))] * 2,
            scratch=[pltpu.VMEM((2, 4 * held, width), BF16)],
            flops=32 * held * width * units,
            moved=10 << 20,
        )(at, came, gate_weight, up_weight)
        got = along_section(send, 0, 1)
        sums = call(join_kernel, shape(4, 2, held, units), [VMEM] * 2, moved=3 << 20)(keep, got)
        terms = swap_y(sums)
        hidden = call(silu_kernel, shape(4, held, units), [VMEM], moved=1 << 20)(terms)
        parts = swap_y(hidden)
        others = along_section(parts, 0, 1)
        out = call(
            functools.partial(down_kernel, held),
            shape(4, 2, held, width),
            [SMEM]
            + [pl.BlockSpec((4, held, units), lambda i: (0, 0, 0))] * 2
            + [pl.BlockSpec((1, units, width), lambda i: (i, 0, 0))],
            grid=(2,),
            out_specs=pl.BlockSpec((4, 1, held, width), lambda i: (0, i, 0, 0)),
            scratch=[pltpu.VMEM((2, 4 * held, units), BF16)],
            flops=16 * held * width * units,
            moved=6 << 20,
        )(at, parts, others, down_weight)
        back = swap_x(out)
        mixed = call(
            functools.partial(mix_kernel, held, rows),
            [shape(rows, width)] * nz,
            [VMEM] * 3,
            flops=16 * held * nz * rows * width,
            moved=2 << 20,
        )(back, code, weight)
        partials += [along_expert(m, -d, 0) if d else m for d, m in zip(chunk, mixed)]
    return sum(p.astype(F32) for p in partials).astype(BF16)


def solution(mesh):
    return jax.shard_map(
        body,
        mesh=mesh,
        in_specs=(
            P("expert", "section"),
            P("expert", None),
            P("expert", None),
            P("expert", "section", None),
            P("expert", "section", None),
            P("expert", None, "section"),
        ),
        out_specs=P("expert", "section"),
        check_vma=False,
    )
```

```python
import functools

import jax
import jax.numpy as jnp
from jax import lax
from jax.experimental import pallas as pl
from jax.experimental.pallas import tpu as pltpu
from jax.sharding import PartitionSpec as P

BF16, F32 = jnp.bfloat16, jnp.float32
NX, CORES = 4, 2
CHUNKS = ((1, -1, 2, -2), (0, 4, 3, -3))
VMEM = pl.BlockSpec(memory_space=pltpu.VMEM)
SMEM = pl.BlockSpec(memory_space=pltpu.SMEM)
HBM = pl.BlockSpec(memory_space=pltpu.HBM)


def along_expert(value, dz, dx):
    count = lax.axis_size("expert")
    planes = count // NX
    return lax.ppermute(
        value,
        "expert",
        [(i, (i // NX + dz) % planes * NX + (i % NX + dx) % NX) for i in range(count)],
    )


def along_section(value, dy, flip):
    count = lax.axis_size("section")
    return lax.ppermute(
        value, "section", [(i, (i + CORES * dy) % count ^ flip) for i in range(count)]
    )


def call(kernel, outs, specs=None, grid=(), out_specs=None, scratch=(), limit=20, flops=0, moved=0):
    return pl.pallas_call(
        kernel,
        grid=grid,
        out_shape=outs,
        in_specs=specs,
        out_specs=out_specs or jax.tree.map(lambda _: VMEM, outs),
        scratch_shapes=scratch,
        compiler_params=pltpu.CompilerParams(vmem_limit_bytes=limit << 20),
        cost_estimate=pl.CostEstimate(flops=16 * flops, bytes_accessed=16 * moved, transcendentals=0),
    )


def select_kernel(capacity, rows, at_ref, *refs):
    nz = len(refs) - 3
    blocks, (out_ref, code_ref, weight_ref) = refs[:nz], refs[nz:]
    per_plane = 2 * NX
    row = lax.broadcasted_iota(jnp.int32, (per_plane, rows), 0)
    expert = (at_ref[0] * per_plane + row).astype(F32)
    earlier = (
        lax.broadcasted_iota(jnp.int32, (rows, rows), 0)
        < lax.broadcasted_iota(jnp.int32, (rows, rows), 1)
    ).astype(F32).astype(BF16)
    codes = []
    for n, block in enumerate(blocks):
        info = block[pl.ds(rows, 16), pl.ds(0, rows)].astype(F32)
        named = jnp.zeros((per_plane, rows), F32)
        weight = jnp.zeros((per_plane, rows), F32)
        for k in range(8):
            hit = info[k : k + 1] == expert
            named = named + jnp.where(hit, 1.0, 0.0)
            weight = weight + jnp.where(hit, info[8 + k : 9 + k], 0.0)
        slot = jnp.dot(named.astype(BF16), earlier, preferred_element_type=F32)
        codes.append(jnp.where(named > 0.5, slot + float(n * capacity), -1.0))
        weight_ref[:, pl.ds(n * rows, rows)] = weight
    code = jnp.concatenate(codes, axis=1)
    code_ref[...] = code
    held = nz * capacity
    at = lax.broadcasted_iota(jnp.int32, (held, nz * rows), 0).astype(F32)
    tokens = jnp.concatenate([block[pl.ds(0, rows), :] for block in blocks], axis=0)
    for r in range(NX):
        pick = jnp.concatenate(
            [jnp.where(at == code[2 * r + e : 2 * r + e + 1], 1.0, 0.0) for e in range(2)], axis=0
        ).astype(BF16)
        out_ref[r] = jnp.dot(pick, tokens, preferred_element_type=F32).astype(BF16)


def up_kernel(held, flip, at_ref, rows_ref, gate_ref, up_ref, out_ref, x_ref, w_ref, sems):
    y = at_ref[2]
    expert = (at_ref[1] + flip) % 2
    half = gate_ref.shape[2] // 2
    pieces = [(part, c) for c in range(2) for part in range(2)]

    def fetch(n):
        part, c = pieces[n]
        return pltpu.make_async_copy(
            (gate_ref, up_ref)[part].at[expert, :, pl.ds(c * half, half)], w_ref.at[n], sems.at[n]
        )

    for n in range(4):
        fetch(n).start()
    for r in range(4):
        x_ref[pl.ds(r * held, held), :] = rows_ref[r, pl.ds(pl.multiple_of(expert * held, held), held), :]
    for n, (part, c) in enumerate(pieces):
        fetch(n).wait()
        sums = jnp.dot(x_ref[...], w_ref[n], preferred_element_type=F32).astype(BF16)
        for r in range(4):
            out_ref[(r + 4 - y) % 4, part, :, pl.ds(c * half, half)] = sums[
                r * held : (r + 1) * held
            ]


def join_kernel(keep_ref, got_ref, *outs):
    for q in range(4):
        outs[q][...] = (keep_ref[q].astype(F32) + got_ref[q].astype(F32)).astype(BF16)


def silu_kernel(a_ref, b_ref, c_ref, d_ref, out_ref):
    gate, up = (
        (a_ref[i].astype(F32) + b_ref[i].astype(F32)) + (c_ref[i].astype(F32) + d_ref[i].astype(F32))
        for i in range(2)
    )
    out_ref[...] = (jax.nn.silu(gate) * up).astype(BF16)


def down_kernel(held, at_ref, own_ref, other_ref, down_ref, out_ref, w_ref, sems):
    core, y = at_ref[1], at_ref[2]

    def fetch(n):
        return pltpu.make_async_copy(down_ref.at[(core + n) % 2], w_ref.at[n], sems.at[n])

    for n in range(2):
        fetch(n).start()
    for n, parts_ref in enumerate((own_ref, other_ref)):
        hidden = parts_ref[...].reshape(4 * held, parts_ref.shape[2])
        fetch(n).wait()
        got = jnp.dot(hidden, w_ref[n], preferred_element_type=F32).astype(BF16)
        for q in range(4):
            out_ref[(y + 4 - q) % 4, (core + n) % 2] = got[q * held : (q + 1) * held]


def mix_kernel(held, rows, back_ref, code_ref, weight_ref, *outs):
    width = code_ref.shape[1]
    at = lax.broadcasted_iota(jnp.int32, (held, width), 0).astype(F32)
    share = jnp.concatenate(
        [
            jnp.where(at == code_ref[j : j + 1, :], weight_ref[j : j + 1, :], 0.0)
            for j in range(2 * NX)
        ],
        axis=0,
    ).astype(BF16)
    total = lax.dot_general(
        share,
        back_ref[...].reshape(share.shape[0], back_ref.shape[3]),
        (((0,), (0,)), ((), ())),
        preferred_element_type=F32,
    ).astype(BF16)
    for n, out in enumerate(outs):
        out[...] = total[n * rows : (n + 1) * rows]


def shape(*dims, dtype=BF16):
    return jax.ShapeDtypeStruct(dims, dtype)


def body(tokens, routes, combine, gate_weight, up_weight, down_weight):
    groups = lax.axis_size("expert")
    per_device, width, units = gate_weight.shape
    rows, fanout = routes.shape
    capacity = 3 * rows * fanout // (2 * per_device * groups)
    place, part = lax.axis_index("expert"), lax.axis_index("section")
    at = jnp.stack([place // NX, part % CORES, part // CORES]).astype(jnp.int32)
    planes = groups // NX
    x_groups = [[z * NX + x for x in range(NX)] for z in range(planes)]
    def swap_x(value):
        return lax.all_to_all(value, "expert", 0, 0, axis_index_groups=x_groups, tiled=True)

    gate_weight, up_weight, down_weight = (
        pltpu.with_memory_space_constraint(w, pltpu.HBM)
        for w in (gate_weight, up_weight, down_weight)
    )
    info = jnp.concatenate([routes.T.astype(BF16), combine.T.astype(BF16)], axis=0)
    block = {0: jnp.concatenate([tokens, jnp.pad(info, ((0, 0), (0, width - rows)))], axis=0)}
    for d in (1, -1, 2, -2, 3, -3, 4):
        step = 1 if d > 0 else -1
        block[d] = along_expert(block[d - step], step, 0)

    chosen = []
    for chunk in CHUNKS:
        nz = len(chunk)
        held = nz * capacity
        chosen.append(
            call(
                functools.partial(select_kernel, capacity, rows),
                [shape(4, 2 * held, width)] + [shape(2 * NX, nz * rows, dtype=F32)] * 2,
                [SMEM] + [VMEM] * nz,
                flops=16 * held * nz * rows * width,
                moved=2 << 20,
            )(at, *[block[d] for d in chunk])
        )

    def expand(came, nz):
        held = nz * capacity
        send, keep = (
            call(
                functools.partial(up_kernel, held, flip),
                shape(4, 2, held, units),
                [SMEM, VMEM, HBM, HBM],
                scratch=[
                    pltpu.VMEM((4 * held, width), BF16),
                    pltpu.VMEM((4, width, units // 2), BF16),
                    pltpu.SemaphoreType.DMA((4,)),
                ],
                flops=16 * held * width * units,
                moved=6 << 20,
            )(at, came, gate_weight, up_weight)
            for flip in (1, 0)
        )
        got = along_section(send, 0, 1)
        return call(
            join_kernel, [shape(2, held, units)] * 4, [VMEM] * 2, moved=3 << 20
        )(keep, got)

    def contract(terms, nz):
        held = nz * capacity
        hidden = call(silu_kernel, shape(held, units), [VMEM] * 4, moved=1 << 20)(*terms)
        parts = jnp.stack([along_section(hidden, q, 0) if q else hidden for q in range(4)])
        others = along_section(parts, 0, 1)
        return call(
            functools.partial(down_kernel, held),
            shape(4, 2, held, width),
            [SMEM, VMEM, VMEM, HBM],
            scratch=[pltpu.VMEM((2, units, width), BF16), pltpu.SemaphoreType.DMA((2,))],
            flops=16 * held * width * units,
            moved=6 << 20,
        )(at, parts, others, down_weight)

    def spread(sums):
        return [along_section(sums[q], q, 0) if q else sums[q] for q in range(4)]

    sizes = [len(chunk) for chunk in CHUNKS]
    came = [swap_x(picked) for picked, _, _ in chosen]
    came[0], chosen = lax.optimization_barrier((came[0], chosen))
    terms = []
    for i, nz in enumerate(sizes):
        if i:
            came[i], sums = lax.optimization_barrier((came[i], sums))
        sums = expand(came[i], nz)
        if i:
            terms[i - 1], sums = lax.optimization_barrier((terms[i - 1], sums))
        terms.append(spread(sums))
    partials = []
    for chunk, (_, code, weight), t in zip(CHUNKS, chosen, terms):
        nz = len(chunk)
        back = swap_x(contract(t, nz))
        mixed = call(
            functools.partial(mix_kernel, nz * capacity, rows),
            [shape(rows, width)] * nz,
            [VMEM] * 3,
            flops=16 * nz * capacity * nz * rows * width,
            moved=2 << 20,
        )(back, code, weight)
        partials += [along_expert(m, -d, 0) if d else m for d, m in zip(chunk, mixed)]
    return sum(p.astype(F32) for p in partials).astype(BF16)


def solution(mesh):
    return jax.shard_map(
        body,
        mesh=mesh,
        in_specs=(
            P("expert", "section"),
            P("expert", None),
            P("expert", None),
            P("expert", "section", None),
            P("expert", "section", None),
            P("expert", None, "section"),
        ),
        out_specs=P("expert", "section"),
        check_vma=False,
    )
```

```python
import functools

import jax
import jax.numpy as jnp
from jax import lax
from jax.experimental import pallas as pl
from jax.experimental.pallas import tpu as pltpu
from jax.sharding import PartitionSpec as P

BF16, F32 = jnp.bfloat16, jnp.float32
NX, CORES = 4, 2
CHUNKS = ((1, -1), (2, -2, 3, -3), (0, 4))
VMEM = pl.BlockSpec(memory_space=pltpu.VMEM)
SMEM = pl.BlockSpec(memory_space=pltpu.SMEM)
HBM = pl.BlockSpec(memory_space=pltpu.HBM)


def along_expert(value, dz, dx):
    count = lax.axis_size("expert")
    planes = count // NX
    return lax.ppermute(
        value,
        "expert",
        [(i, (i // NX + dz) % planes * NX + (i % NX + dx) % NX) for i in range(count)],
    )


def along_section(value, dy, flip):
    count = lax.axis_size("section")
    return lax.ppermute(
        value, "section", [(i, (i + CORES * dy) % count ^ flip) for i in range(count)]
    )


def call(kernel, outs, specs=None, grid=(), out_specs=None, scratch=(), limit=20, flops=0, moved=0):
    return pl.pallas_call(
        kernel,
        grid=grid,
        out_shape=outs,
        in_specs=specs,
        out_specs=out_specs or jax.tree.map(lambda _: VMEM, outs),
        scratch_shapes=scratch,
        compiler_params=pltpu.CompilerParams(vmem_limit_bytes=limit << 20),
        cost_estimate=pl.CostEstimate(flops=16 * flops, bytes_accessed=16 * moved, transcendentals=0),
    )


def pack_kernel(rows, tokens_ref, routes_ref, combine_ref, out_ref, t_ref, r_ref, c_ref, sems):
    copies = [
        pltpu.make_async_copy(src, dst, sems.at[n])
        for n, (src, dst) in enumerate(
            ((tokens_ref, t_ref), (routes_ref, r_ref), (combine_ref, c_ref))
        )
    ]
    for copy in copies:
        copy.start()
    for copy in copies:
        copy.wait()
    out_ref[pl.ds(0, rows), :] = t_ref[...]
    info = jnp.concatenate([r_ref[...].astype(F32), c_ref[...]], axis=0)
    rest = jnp.zeros((info.shape[0], out_ref.shape[1] - rows), F32)
    out_ref[pl.ds(rows, 16), :] = jnp.concatenate([info, rest], axis=1).astype(BF16)


def select_kernel(capacity, rows, at_ref, *refs):
    nz = len(refs) - 3
    blocks, (out_ref, code_ref, weight_ref) = refs[:nz], refs[nz:]
    per_plane = 2 * NX
    row = lax.broadcasted_iota(jnp.int32, (per_plane, rows), 0)
    expert = (at_ref[0] * per_plane + row).astype(F32)
    earlier = (
        lax.broadcasted_iota(jnp.int32, (rows, rows), 0)
        < lax.broadcasted_iota(jnp.int32, (rows, rows), 1)
    ).astype(F32).astype(BF16)
    codes = []
    for n, block in enumerate(blocks):
        info = block[pl.ds(rows, 16), pl.ds(0, rows)].astype(F32)
        named = jnp.zeros((per_plane, rows), F32)
        weight = jnp.zeros((per_plane, rows), F32)
        for k in range(8):
            hit = info[k : k + 1] == expert
            named = named + jnp.where(hit, 1.0, 0.0)
            weight = weight + jnp.where(hit, info[8 + k : 9 + k], 0.0)
        slot = jnp.dot(named.astype(BF16), earlier, preferred_element_type=F32)
        codes.append(jnp.where(named > 0.5, slot + float(n * capacity), -1.0))
        weight_ref[:, pl.ds(n * rows, rows)] = weight
    code = jnp.concatenate(codes, axis=1)
    code_ref[...] = code
    held = nz * capacity
    at = lax.broadcasted_iota(jnp.int32, (held, nz * rows), 0).astype(F32)
    tokens = jnp.concatenate([block[pl.ds(0, rows), :] for block in blocks], axis=0)
    for r in range(NX):
        pick = jnp.concatenate(
            [jnp.where(at == code[2 * r + e : 2 * r + e + 1], 1.0, 0.0) for e in range(2)], axis=0
        ).astype(BF16)
        out_ref[r] = jnp.dot(pick, tokens, preferred_element_type=F32).astype(BF16)


def up_kernel(held, flip, at_ref, rows_ref, gate_ref, up_ref, out_ref, x_ref, w_ref, sems):
    y = at_ref[2]
    expert = (at_ref[1] + flip) % 2
    half = gate_ref.shape[2] // 2
    pieces = [(part, c) for c in range(2) for part in range(2)]

    def fetch(n):
        part, c = pieces[n]
        return pltpu.make_async_copy(
            (gate_ref, up_ref)[part].at[expert, :, pl.ds(c * half, half)], w_ref.at[n], sems.at[n]
        )

    for n in range(4):
        fetch(n).start()
    for r in range(4):
        x_ref[pl.ds(r * held, held), :] = rows_ref[r, pl.ds(pl.multiple_of(expert * held, held), held), :]
    for n, (part, c) in enumerate(pieces):
        fetch(n).wait()
        sums = jnp.dot(x_ref[...], w_ref[n], preferred_element_type=F32).astype(BF16)
        for r in range(4):
            out_ref[(r + 4 - y) % 4, part, :, pl.ds(c * half, half)] = sums[
                r * held : (r + 1) * held
            ]


def join_kernel(keep_ref, got_ref, *outs):
    for q in range(4):
        outs[q][...] = (keep_ref[q].astype(F32) + got_ref[q].astype(F32)).astype(BF16)


def silu_kernel(a_ref, b_ref, c_ref, d_ref, out_ref):
    gate, up = (
        (a_ref[i].astype(F32) + b_ref[i].astype(F32)) + (c_ref[i].astype(F32) + d_ref[i].astype(F32))
        for i in range(2)
    )
    out_ref[...] = (jax.nn.silu(gate) * up).astype(BF16)


def down_kernel(held, at_ref, own_ref, other_ref, down_ref, out_ref, w_ref, sems):
    core, y = at_ref[1], at_ref[2]

    def fetch(n):
        return pltpu.make_async_copy(down_ref.at[(core + n) % 2], w_ref.at[n], sems.at[n])

    for n in range(2):
        fetch(n).start()
    for n, parts_ref in enumerate((own_ref, other_ref)):
        hidden = parts_ref[...].reshape(4 * held, parts_ref.shape[2])
        fetch(n).wait()
        got = jnp.dot(hidden, w_ref[n], preferred_element_type=F32).astype(BF16)
        for q in range(4):
            out_ref[(y + 4 - q) % 4, (core + n) % 2] = got[q * held : (q + 1) * held]


def mix_kernel(held, rows, back_ref, code_ref, weight_ref, *outs):
    width = code_ref.shape[1]
    at = lax.broadcasted_iota(jnp.int32, (held, width), 0).astype(F32)
    share = jnp.concatenate(
        [
            jnp.where(at == code_ref[j : j + 1, :], weight_ref[j : j + 1, :], 0.0)
            for j in range(2 * NX)
        ],
        axis=0,
    ).astype(BF16)
    total = lax.dot_general(
        share,
        back_ref[...].reshape(share.shape[0], back_ref.shape[3]),
        (((0,), (0,)), ((), ())),
        preferred_element_type=F32,
    ).astype(BF16)
    for n, out in enumerate(outs):
        out[...] = total[n * rows : (n + 1) * rows]


def shape(*dims, dtype=BF16):
    return jax.ShapeDtypeStruct(dims, dtype)


def body(tokens, routes, combine, gate_weight, up_weight, down_weight):
    groups = lax.axis_size("expert")
    per_device, width, units = gate_weight.shape
    rows, fanout = routes.shape
    capacity = 3 * rows * fanout // (2 * per_device * groups)
    place, part = lax.axis_index("expert"), lax.axis_index("section")
    at = jnp.stack([place // NX, part % CORES, part // CORES]).astype(jnp.int32)
    planes = groups // NX
    x_groups = [[z * NX + x for x in range(NX)] for z in range(planes)]
    def swap_x(value):
        return lax.all_to_all(value, "expert", 0, 0, axis_index_groups=x_groups, tiled=True)

    gate_weight, up_weight, down_weight = (
        pltpu.with_memory_space_constraint(w, pltpu.HBM)
        for w in (gate_weight, up_weight, down_weight)
    )
    block = {
        0: call(
            functools.partial(pack_kernel, rows),
            shape(rows + 16, width),
            [HBM] * 3,
            scratch=[
                pltpu.VMEM((rows, width), BF16),
                pltpu.VMEM((fanout, rows), jnp.int32),
                pltpu.VMEM((fanout, rows), F32),
                pltpu.SemaphoreType.DMA((3,)),
            ],
            moved=1 << 19,
        )(*(pltpu.with_memory_space_constraint(v, pltpu.HBM) for v in (tokens, routes.T, combine.T)))
    }
    for d in (1, -1, 2, -2):
        step = 1 if d > 0 else -1
        block[d] = along_expert(block[d - step], step, 0)
    chosen = []
    for chunk in CHUNKS:
        nz = len(chunk)
        held = nz * capacity
        if chunk == CHUNKS[1]:
            (block[2], block[-2]), chosen = lax.optimization_barrier(
                ((block[2], block[-2]), chosen)
            )
            for d in (3, -3, 4):
                step = 1 if d > 0 else -1
                block[d] = along_expert(block[d - step], step, 0)
        chosen.append(
            call(
                functools.partial(select_kernel, capacity, rows),
                [shape(4, 2 * held, width)] + [shape(2 * NX, nz * rows, dtype=F32)] * 2,
                [SMEM] + [VMEM] * nz,
                flops=16 * held * nz * rows * width,
                moved=2 << 20,
            )(at, *[block[d] for d in chunk])
        )

    def expand(came, nz):
        held = nz * capacity
        send, keep = (
            call(
                functools.partial(up_kernel, held, flip),
                shape(4, 2, held, units),
                [SMEM, VMEM, HBM, HBM],
                scratch=[
                    pltpu.VMEM((4 * held, width), BF16),
                    pltpu.VMEM((4, width, units // 2), BF16),
                    pltpu.SemaphoreType.DMA((4,)),
                ],
                flops=16 * held * width * units,
                moved=6 << 20,
            )(at, came, gate_weight, up_weight)
            for flip in (1, 0)
        )
        got = along_section(send, 0, 1)
        return call(
            join_kernel, [shape(2, held, units)] * 4, [VMEM] * 2, moved=3 << 20
        )(keep, got)

    def spread(sums):
        return [along_section(sums[q], q, 0) if q else sums[q] for q in range(4)]

    sizes = [len(chunk) for chunk in CHUNKS]
    came = [swap_x(picked) for picked, _, _ in chosen]
    terms = []
    for i, nz in enumerate(sizes):
        if i:
            came[i], sums = lax.optimization_barrier((came[i], sums))
        sums = expand(came[i], nz)
        if i:
            terms[i - 1], sums = lax.optimization_barrier((terms[i - 1], sums))
        terms.append(spread(sums))
    def activate(terms, nz):
        return call(
            silu_kernel, shape(nz * capacity, units), [VMEM] * 4, moved=1 << 20
        )(*terms)

    partials, back, hidden = [], (), activate(terms[0], sizes[0])
    for i, (chunk, (_, code, weight), nz) in enumerate(zip(CHUNKS, chosen, sizes)):
        held = nz * capacity
        pieces = [along_section(hidden, q, 0) if q else hidden for q in range(4)]
        if i + 1 < len(sizes):
            pieces, terms[i + 1], back = lax.optimization_barrier((pieces, terms[i + 1], back))
        parts = jnp.stack(pieces)
        others = along_section(parts, 0, 1)
        if i + 1 < len(sizes):
            hidden = activate(terms[i + 1], sizes[i + 1])
            parts, hidden = lax.optimization_barrier((parts, hidden))
        else:
            parts, others, back = lax.optimization_barrier((parts, others, back))
        out = call(
            functools.partial(down_kernel, held),
            shape(4, 2, held, width),
            [SMEM, VMEM, VMEM, HBM],
            scratch=[pltpu.VMEM((2, units, width), BF16), pltpu.SemaphoreType.DMA((2,))],
            flops=16 * held * width * units,
            moved=6 << 20,
        )(at, parts, others, down_weight)
        back = swap_x(out)
        mixed = call(
            functools.partial(mix_kernel, held, rows),
            [shape(rows, width)] * nz,
            [VMEM] * 3,
            flops=16 * held * nz * rows * width,
            moved=2 << 20,
        )(back, code, weight)
        partials += [along_expert(m, -d, 0) if d else m for d, m in zip(chunk, mixed)]
    return sum(p.astype(F32) for p in partials).astype(BF16)


def solution(mesh):
    return jax.shard_map(
        body,
        mesh=mesh,
        in_specs=(
            P("expert", "section"),
            P("expert", None),
            P("expert", None),
            P("expert", "section", None),
            P("expert", "section", None),
            P("expert", None, "section"),
        ),
        out_specs=P("expert", "section"),
        check_vma=False,
    )
```

```python
import functools

import jax
import jax.numpy as jnp
from jax import lax
from jax.experimental import pallas as pl
from jax.experimental.pallas import tpu as pltpu
from jax.sharding import PartitionSpec as P

BF16, F32 = jnp.bfloat16, jnp.float32
NX, CORES = 4, 2
CHUNKS = ((1, -1, 2, -2), (0, 4, 3, -3))
VMEM = pl.BlockSpec(memory_space=pltpu.VMEM)
SMEM = pl.BlockSpec(memory_space=pltpu.SMEM)
HBM = pl.BlockSpec(memory_space=pltpu.HBM)


def along_expert(value, dz, dx):
    count = lax.axis_size("expert")
    planes = count // NX
    return lax.ppermute(
        value,
        "expert",
        [(i, (i // NX + dz) % planes * NX + (i % NX + dx) % NX) for i in range(count)],
    )


def along_section(value, dy, flip):
    count = lax.axis_size("section")
    return lax.ppermute(
        value, "section", [(i, (i + CORES * dy) % count ^ flip) for i in range(count)]
    )


def call(kernel, outs, specs=None, grid=(), out_specs=None, scratch=(), limit=20, flops=0, moved=0):
    return pl.pallas_call(
        kernel,
        grid=grid,
        out_shape=outs,
        in_specs=specs,
        out_specs=out_specs or jax.tree.map(lambda _: VMEM, outs),
        scratch_shapes=scratch,
        compiler_params=pltpu.CompilerParams(vmem_limit_bytes=limit << 20),
        cost_estimate=pl.CostEstimate(flops=16 * flops, bytes_accessed=16 * moved, transcendentals=0),
    )


def pack_kernel(rows, tokens_ref, routes_ref, combine_ref, out_ref, t_ref, r_ref, c_ref, sems):
    copies = [
        pltpu.make_async_copy(src, dst, sems.at[n])
        for n, (src, dst) in enumerate(
            ((tokens_ref, t_ref), (routes_ref, r_ref), (combine_ref, c_ref))
        )
    ]
    for copy in copies:
        copy.start()
    for copy in copies:
        copy.wait()
    out_ref[pl.ds(0, rows), :] = t_ref[...]
    info = jnp.concatenate([r_ref[...].astype(F32), c_ref[...]], axis=0)
    rest = jnp.zeros((info.shape[0], out_ref.shape[1] - rows), F32)
    out_ref[pl.ds(rows, 16), :] = jnp.concatenate([info, rest], axis=1).astype(BF16)


def select_kernel(capacity, rows, at_ref, *refs):
    nz = len(refs) - 3
    blocks, (out_ref, code_ref, weight_ref) = refs[:nz], refs[nz:]
    per_plane = 2 * NX
    row = lax.broadcasted_iota(jnp.int32, (per_plane, rows), 0)
    expert = (at_ref[0] * per_plane + row).astype(F32)
    earlier = (
        lax.broadcasted_iota(jnp.int32, (rows, rows), 0)
        < lax.broadcasted_iota(jnp.int32, (rows, rows), 1)
    ).astype(F32).astype(BF16)
    codes = []
    for n, block in enumerate(blocks):
        info = block[pl.ds(rows, 16), pl.ds(0, rows)].astype(F32)
        named = jnp.zeros((per_plane, rows), F32)
        weight = jnp.zeros((per_plane, rows), F32)
        for k in range(8):
            hit = info[k : k + 1] == expert
            named = named + jnp.where(hit, 1.0, 0.0)
            weight = weight + jnp.where(hit, info[8 + k : 9 + k], 0.0)
        slot = jnp.dot(named.astype(BF16), earlier, preferred_element_type=F32)
        codes.append(jnp.where(named > 0.5, slot + float(n * capacity), -1.0))
        weight_ref[:, pl.ds(n * rows, rows)] = weight
    code = jnp.concatenate(codes, axis=1)
    code_ref[...] = code
    held = nz * capacity
    at = lax.broadcasted_iota(jnp.int32, (held, nz * rows), 0).astype(F32)
    tokens = jnp.concatenate([block[pl.ds(0, rows), :] for block in blocks], axis=0)
    for r in range(NX):
        pick = jnp.concatenate(
            [jnp.where(at == code[2 * r + e : 2 * r + e + 1], 1.0, 0.0) for e in range(2)], axis=0
        ).astype(BF16)
        out_ref[r] = jnp.dot(pick, tokens, preferred_element_type=F32).astype(BF16)


def up_kernel(held, flip, at_ref, rows_ref, gate_ref, up_ref, out_ref, x_ref, w_ref, sems):
    y = at_ref[2]
    expert = (at_ref[1] + flip) % 2
    half = gate_ref.shape[2] // 2
    pieces = [(part, c) for c in range(2) for part in range(2)]

    def fetch(n):
        part, c = pieces[n]
        return pltpu.make_async_copy(
            (gate_ref, up_ref)[part].at[expert, :, pl.ds(c * half, half)], w_ref.at[n], sems.at[n]
        )

    for n in range(4):
        fetch(n).start()
    for r in range(4):
        x_ref[pl.ds(r * held, held), :] = rows_ref[r, pl.ds(pl.multiple_of(expert * held, held), held), :]
    for n, (part, c) in enumerate(pieces):
        fetch(n).wait()
        sums = jnp.dot(x_ref[...], w_ref[n], preferred_element_type=F32).astype(BF16)
        for r in range(4):
            out_ref[(r + 4 - y) % 4, part, :, pl.ds(c * half, half)] = sums[
                r * held : (r + 1) * held
            ]


def join_kernel(keep_ref, got_ref, *outs):
    for q in range(4):
        outs[q][...] = (keep_ref[q].astype(F32) + got_ref[q].astype(F32)).astype(BF16)


def silu_kernel(a_ref, b_ref, c_ref, d_ref, out_ref):
    gate, up = (
        (a_ref[i].astype(F32) + b_ref[i].astype(F32)) + (c_ref[i].astype(F32) + d_ref[i].astype(F32))
        for i in range(2)
    )
    out_ref[...] = (jax.nn.silu(gate) * up).astype(BF16)


def down_kernel(held, at_ref, own_ref, other_ref, down_ref, out_ref, w_ref, sems):
    core, y = at_ref[1], at_ref[2]

    def fetch(n):
        return pltpu.make_async_copy(down_ref.at[(core + n) % 2], w_ref.at[n], sems.at[n])

    for n in range(2):
        fetch(n).start()
    for n, parts_ref in enumerate((own_ref, other_ref)):
        hidden = parts_ref[...].reshape(4 * held, parts_ref.shape[2])
        fetch(n).wait()
        got = jnp.dot(hidden, w_ref[n], preferred_element_type=F32).astype(BF16)
        for q in range(4):
            out_ref[(y + 4 - q) % 4, (core + n) % 2] = got[q * held : (q + 1) * held]


def mix_kernel(held, rows, back_ref, code_ref, weight_ref, *outs):
    width = code_ref.shape[1]
    at = lax.broadcasted_iota(jnp.int32, (held, width), 0).astype(F32)
    share = jnp.concatenate(
        [
            jnp.where(at == code_ref[j : j + 1, :], weight_ref[j : j + 1, :], 0.0)
            for j in range(2 * NX)
        ],
        axis=0,
    ).astype(BF16)
    total = lax.dot_general(
        share,
        back_ref[...].reshape(share.shape[0], back_ref.shape[3]),
        (((0,), (0,)), ((), ())),
        preferred_element_type=F32,
    ).astype(BF16)
    for n, out in enumerate(outs):
        out[...] = total[n * rows : (n + 1) * rows]


def shape(*dims, dtype=BF16):
    return jax.ShapeDtypeStruct(dims, dtype)


def body(tokens, routes, combine, gate_weight, up_weight, down_weight):
    groups = lax.axis_size("expert")
    per_device, width, units = gate_weight.shape
    rows, fanout = routes.shape
    capacity = 3 * rows * fanout // (2 * per_device * groups)
    place, part = lax.axis_index("expert"), lax.axis_index("section")
    at = jnp.stack([place // NX, part % CORES, part // CORES]).astype(jnp.int32)
    planes = groups // NX
    x_groups = [[z * NX + x for x in range(NX)] for z in range(planes)]
    def swap_x(value):
        return lax.all_to_all(value, "expert", 0, 0, axis_index_groups=x_groups, tiled=True)

    gate_weight, up_weight, down_weight = (
        pltpu.with_memory_space_constraint(w, pltpu.HBM)
        for w in (gate_weight, up_weight, down_weight)
    )
    block = {
        0: call(
            functools.partial(pack_kernel, rows),
            shape(rows + 16, width),
            [HBM] * 3,
            scratch=[
                pltpu.VMEM((rows, width), BF16),
                pltpu.VMEM((fanout, rows), jnp.int32),
                pltpu.VMEM((fanout, rows), F32),
                pltpu.SemaphoreType.DMA((3,)),
            ],
            moved=1 << 19,
        )(*(pltpu.with_memory_space_constraint(v, pltpu.HBM) for v in (tokens, routes.T, combine.T)))
    }
    for d in (1, -1, 2, -2):
        step = 1 if d > 0 else -1
        block[d] = along_expert(block[d - step], step, 0)
    chosen = []
    for chunk in CHUNKS:
        nz = len(chunk)
        held = nz * capacity
        if chunk == CHUNKS[1]:
            own, ahead, behind, chosen = lax.optimization_barrier(
                (block[0], block[2], block[-2], chosen)
            )
            block[3], block[-3] = along_expert(ahead, 1, 0), along_expert(behind, -1, 0)
            block[4] = along_expert(own, 4, 0)
        chosen.append(
            call(
                functools.partial(select_kernel, capacity, rows),
                [shape(4, 2 * held, width)] + [shape(2 * NX, nz * rows, dtype=F32)] * 2,
                [SMEM] + [VMEM] * nz,
                flops=16 * held * nz * rows * width,
                moved=2 << 20,
            )(at, *[block[d] for d in chunk])
        )

    def expand(came, nz):
        held = nz * capacity
        send, keep = (
            call(
                functools.partial(up_kernel, held, flip),
                shape(4, 2, held, units),
                [SMEM, VMEM, HBM, HBM],
                scratch=[
                    pltpu.VMEM((4 * held, width), BF16),
                    pltpu.VMEM((4, width, units // 2), BF16),
                    pltpu.SemaphoreType.DMA((4,)),
                ],
                flops=16 * held * width * units,
                moved=6 << 20,
            )(at, came, gate_weight, up_weight)
            for flip in (1, 0)
        )
        got = along_section(send, 0, 1)
        return call(
            join_kernel, [shape(2, held, units)] * 4, [VMEM] * 2, moved=3 << 20
        )(keep, got)

    def spread(sums):
        return [along_section(sums[q], q, 0) if q else sums[q] for q in range(4)]

    sizes = [len(chunk) for chunk in CHUNKS]
    came = [swap_x(picked) for picked, _, _ in chosen]
    terms = []
    for i, nz in enumerate(sizes):
        if i:
            came[i], sums = lax.optimization_barrier((came[i], sums))
        sums = expand(came[i], nz)
        if i:
            terms[i - 1], sums = lax.optimization_barrier((terms[i - 1], sums))
        terms.append(spread(sums))
    def activate(terms, nz):
        return call(
            silu_kernel, shape(nz * capacity, units), [VMEM] * 4, moved=1 << 20
        )(*terms)

    partials, back, hidden = [], (), activate(terms[0], sizes[0])
    for i, (chunk, (_, code, weight), nz) in enumerate(zip(CHUNKS, chosen, sizes)):
        held = nz * capacity
        pieces = [along_section(hidden, q, 0) if q else hidden for q in range(4)]
        if i + 1 < len(sizes):
            pieces, terms[i + 1], back = lax.optimization_barrier((pieces, terms[i + 1], back))
        if i:
            pieces, out = lax.optimization_barrier((pieces, out))
        parts = jnp.stack(pieces)
        others = along_section(parts, 0, 1)
        if i + 1 < len(sizes):
            hidden = activate(terms[i + 1], sizes[i + 1])
            parts, hidden = lax.optimization_barrier((parts, hidden))
        out = call(
            functools.partial(down_kernel, held),
            shape(4, 2, held, width),
            [SMEM, VMEM, VMEM, HBM],
            scratch=[pltpu.VMEM((2, units, width), BF16), pltpu.SemaphoreType.DMA((2,))],
            moved=1 << 10,
        )(at, parts, others, down_weight)
        back = swap_x(out)
        mixed = call(
            functools.partial(mix_kernel, held, rows),
            [shape(rows, width)] * nz,
            [VMEM] * 3,
            flops=16 * held * nz * rows * width,
            moved=2 << 20,
        )(back, code, weight)
        partials += [along_expert(m, -d, 0) if d else m for d, m in zip(chunk, mixed)]
    return sum(p.astype(F32) for p in partials).astype(BF16)


def solution(mesh):
    return jax.shard_map(
        body,
        mesh=mesh,
        in_specs=(
            P("expert", "section"),
            P("expert", None),
            P("expert", None),
            P("expert", "section", None),
            P("expert", "section", None),
            P("expert", None, "section"),
        ),
        out_specs=P("expert", "section"),
        check_vma=False,
    )
```

```python
import functools

import jax
import jax.numpy as jnp
from jax import lax
from jax.experimental import pallas as pl
from jax.experimental.pallas import tpu as pltpu
from jax.sharding import PartitionSpec as P

BF16, F32 = jnp.bfloat16, jnp.float32
NX, CORES = 4, 2
CHUNKS = ((1, -1, 2, -2), (0, 4, 3, -3))
VMEM = pl.BlockSpec(memory_space=pltpu.VMEM)
SMEM = pl.BlockSpec(memory_space=pltpu.SMEM)
HBM = pl.BlockSpec(memory_space=pltpu.HBM)


def along_expert(value, dz, dx):
    count = lax.axis_size("expert")
    planes = count // NX
    return lax.ppermute(
        value,
        "expert",
        [(i, (i // NX + dz) % planes * NX + (i % NX + dx) % NX) for i in range(count)],
    )


def along_section(value, dy, flip):
    count = lax.axis_size("section")
    return lax.ppermute(
        value, "section", [(i, (i + CORES * dy) % count ^ flip) for i in range(count)]
    )


def call(kernel, outs, specs=None, grid=(), out_specs=None, scratch=(), limit=20, flops=0, moved=0):
    return pl.pallas_call(
        kernel,
        grid=grid,
        out_shape=outs,
        in_specs=specs,
        out_specs=out_specs or jax.tree.map(lambda _: VMEM, outs),
        scratch_shapes=scratch,
        compiler_params=pltpu.CompilerParams(vmem_limit_bytes=limit << 20),
        cost_estimate=pl.CostEstimate(flops=16 * flops, bytes_accessed=16 * moved, transcendentals=0),
    )


def pack_kernel(rows, tokens_ref, routes_ref, combine_ref, out_ref, t_ref, r_ref, c_ref, sems):
    copies = [
        pltpu.make_async_copy(src, dst, sems.at[n])
        for n, (src, dst) in enumerate(
            ((tokens_ref, t_ref), (routes_ref, r_ref), (combine_ref, c_ref))
        )
    ]
    for copy in copies:
        copy.start()
    for copy in copies:
        copy.wait()
    out_ref[pl.ds(0, rows), :] = t_ref[...]
    info = jnp.concatenate([r_ref[...].astype(F32), c_ref[...]], axis=0)
    rest = jnp.zeros((info.shape[0], out_ref.shape[1] - rows), F32)
    out_ref[pl.ds(rows, 16), :] = jnp.concatenate([info, rest], axis=1).astype(BF16)


def select_kernel(capacity, rows, at_ref, *refs):
    nz = len(refs) - 3
    blocks, (out_ref, code_ref, weight_ref) = refs[:nz], refs[nz:]
    per_plane = 2 * NX
    row = lax.broadcasted_iota(jnp.int32, (per_plane, rows), 0)
    expert = (at_ref[0] * per_plane + row).astype(F32)
    earlier = (
        lax.broadcasted_iota(jnp.int32, (rows, rows), 0)
        < lax.broadcasted_iota(jnp.int32, (rows, rows), 1)
    ).astype(F32).astype(BF16)
    codes = []
    for n, block in enumerate(blocks):
        info = block[pl.ds(rows, 16), pl.ds(0, rows)].astype(F32)
        named = jnp.zeros((per_plane, rows), F32)
        weight = jnp.zeros((per_plane, rows), F32)
        for k in range(8):
            hit = info[k : k + 1] == expert
            named = named + jnp.where(hit, 1.0, 0.0)
            weight = weight + jnp.where(hit, info[8 + k : 9 + k], 0.0)
        slot = jnp.dot(named.astype(BF16), earlier, preferred_element_type=F32)
        codes.append(jnp.where(named > 0.5, slot + float(n * capacity), -1.0))
        weight_ref[:, pl.ds(n * rows, rows)] = weight
    code = jnp.concatenate(codes, axis=1)
    code_ref[...] = code
    held = nz * capacity
    at = lax.broadcasted_iota(jnp.int32, (held, nz * rows), 0).astype(F32)
    tokens = jnp.concatenate([block[pl.ds(0, rows), :] for block in blocks], axis=0)
    for r in range(NX):
        pick = jnp.concatenate(
            [jnp.where(at == code[2 * r + e : 2 * r + e + 1], 1.0, 0.0) for e in range(2)], axis=0
        ).astype(BF16)
        out_ref[r] = jnp.dot(pick, tokens, preferred_element_type=F32).astype(BF16)


def up_kernel(held, flip, at_ref, rows_ref, gate_ref, up_ref, out_ref, x_ref, w_ref, sems):
    y = at_ref[2]
    expert = (at_ref[1] + flip) % 2
    half = gate_ref.shape[2] // 2
    pieces = [(part, c) for c in range(2) for part in range(2)]

    def fetch(n):
        part, c = pieces[n]
        return pltpu.make_async_copy(
            (gate_ref, up_ref)[part].at[expert, :, pl.ds(c * half, half)], w_ref.at[n], sems.at[n]
        )

    for n in range(4):
        fetch(n).start()
    for r in range(4):
        x_ref[pl.ds(r * held, held), :] = rows_ref[r, pl.ds(pl.multiple_of(expert * held, held), held), :]
    for n, (part, c) in enumerate(pieces):
        fetch(n).wait()
        sums = jnp.dot(x_ref[...], w_ref[n], preferred_element_type=F32).astype(BF16)
        for r in range(4):
            out_ref[(r + 4 - y) % 4, part, :, pl.ds(c * half, half)] = sums[
                r * held : (r + 1) * held
            ]


def join_kernel(keep_ref, got_ref, *outs):
    for q in range(4):
        outs[q][...] = (keep_ref[q].astype(F32) + got_ref[q].astype(F32)).astype(BF16)


def activate(terms):
    gate, up = (
        (terms[0][i].astype(F32) + terms[1][i].astype(F32))
        + (terms[2][i].astype(F32) + terms[3][i].astype(F32))
        for i in range(2)
    )
    return (jax.nn.silu(gate) * up).astype(BF16)


def silu_kernel(*refs):
    refs[4][...] = activate(refs[:4])


def turn_kernel(*refs):
    terms, (keep_ref, got_ref), outs = refs[:4], refs[4:6], refs[6:]
    hidden = activate(terms)
    for q in range(4):
        outs[q][pl.ds(0, 2)] = (keep_ref[q].astype(F32) + got_ref[q].astype(F32)).astype(BF16)
        outs[q][2] = hidden


def down_kernel(held, at_ref, own_ref, other_ref, down_ref, *refs):
    outs, (h_ref, w_ref, sems) = refs[:4], refs[4:]
    core, y, x = at_ref[1], at_ref[2], at_ref[3]

    def fetch(n):
        return pltpu.make_async_copy(down_ref.at[(core + n) % 2], w_ref.at[n], sems.at[n])

    for n in range(2):
        fetch(n).start()
    for n, parts_ref in enumerate((own_ref, other_ref)):
        for d in range(4):
            h_ref[pl.ds(d * held, held), :] = parts_ref[(y + 8 - x - d) % 4]
        fetch(n).wait()
        got = jnp.dot(h_ref[...], w_ref[n], preferred_element_type=F32).astype(BF16)
        for d in range(4):
            outs[d][(core + n) % 2] = got[d * held : (d + 1) * held]


def mix_kernel(held, rows, at_ref, *refs):
    backs, (code_ref, weight_ref), outs = refs[:4], refs[4:6], refs[6:]
    width = code_ref.shape[1]
    at = lax.broadcasted_iota(jnp.int32, (held, width), 0).astype(F32)
    share = []
    for d in range(4):
        for e in range(2):
            j = pl.ds((at_ref[3] + 4 - d) % 4 * 2 + e, 1)
            share.append(jnp.where(at == code_ref[j, :], weight_ref[j, :], 0.0))
    back = jnp.concatenate([backs[d][e] for d in range(4) for e in range(2)], axis=0)
    total = lax.dot_general(
        jnp.concatenate(share, axis=0).astype(BF16),
        back,
        (((0,), (0,)), ((), ())),
        preferred_element_type=F32,
    ).astype(BF16)
    for n, out in enumerate(outs):
        out[...] = total[n * rows : (n + 1) * rows]


def shape(*dims, dtype=BF16):
    return jax.ShapeDtypeStruct(dims, dtype)


def body(tokens, routes, combine, gate_weight, up_weight, down_weight):
    groups = lax.axis_size("expert")
    per_device, width, units = gate_weight.shape
    rows, fanout = routes.shape
    capacity = 3 * rows * fanout // (2 * per_device * groups)
    place, part = lax.axis_index("expert"), lax.axis_index("section")
    at = jnp.stack([place // NX, part % CORES, part // CORES, place % NX]).astype(jnp.int32)
    planes = groups // NX
    x_groups = [[z * NX + x for x in range(NX)] for z in range(planes)]
    def swap_x(value):
        return lax.all_to_all(value, "expert", 0, 0, axis_index_groups=x_groups, tiled=True)

    gate_weight, up_weight, down_weight = (
        pltpu.with_memory_space_constraint(w, pltpu.HBM)
        for w in (gate_weight, up_weight, down_weight)
    )
    block = {
        0: call(
            functools.partial(pack_kernel, rows),
            shape(rows + 16, width),
            [HBM] * 3,
            scratch=[
                pltpu.VMEM((rows, width), BF16),
                pltpu.VMEM((fanout, rows), jnp.int32),
                pltpu.VMEM((fanout, rows), F32),
                pltpu.SemaphoreType.DMA((3,)),
            ],
            moved=1 << 19,
        )(*(pltpu.with_memory_space_constraint(v, pltpu.HBM) for v in (tokens, routes.T, combine.T)))
    }
    for d in (1, -1, 2, -2):
        step = 1 if d > 0 else -1
        block[d] = along_expert(block[d - step], step, 0)
    chosen = []
    for chunk in CHUNKS:
        nz = len(chunk)
        held = nz * capacity
        if chunk == CHUNKS[1]:
            own, ahead, behind, chosen = lax.optimization_barrier(
                (block[0], block[2], block[-2], chosen)
            )
            block[3], block[-3] = along_expert(ahead, 1, 0), along_expert(behind, -1, 0)
            block[4] = along_expert(own, 4, 0)
        chosen.append(
            call(
                functools.partial(select_kernel, capacity, rows),
                [shape(4, 2 * held, width)] + [shape(2 * NX, nz * rows, dtype=F32)] * 2,
                [SMEM] + [VMEM] * nz,
                flops=16 * held * nz * rows * width,
                moved=2 << 20,
            )(at, *[block[d] for d in chunk])
        )

    def expand(came):
        send, keep = (
            call(
                functools.partial(up_kernel, held, flip),
                shape(4, 2, held, units),
                [SMEM, VMEM, HBM, HBM],
                scratch=[
                    pltpu.VMEM((4 * held, width), BF16),
                    pltpu.VMEM((4, width, units // 2), BF16),
                    pltpu.SemaphoreType.DMA((4,)),
                ],
                flops=16 * held * width * units,
                moved=6 << 20,
            )(at, came, gate_weight, up_weight)
            for flip in (1, 0)
        )
        return keep, along_section(send, 0, 1)

    def spread(values):
        return [along_section(v, q, 0) if q else v for q, v in enumerate(values)]

    def contract(parts, others):
        out = call(
            functools.partial(down_kernel, held),
            [shape(2, held, width)] * 4,
            [SMEM, VMEM, VMEM, HBM],
            scratch=[
                pltpu.VMEM((4 * held, units), BF16),
                pltpu.VMEM((2, units, width), BF16),
                pltpu.SemaphoreType.DMA((2,)),
            ],
            moved=1 << 10,
        )(at, parts, others, down_weight)
        return out, [along_expert(v, 0, d) if d else v for d, v in enumerate(out)]

    def mix(chunk, back, code, weight):
        mixed = call(
            functools.partial(mix_kernel, held, rows),
            [shape(rows, width)] * len(chunk),
            [SMEM] + [VMEM] * 6,
            flops=16 * held * len(chunk) * rows * width,
            moved=2 << 20,
        )(at, *back, code, weight)
        return [along_expert(m, -d, 0) if d else m for d, m in zip(chunk, mixed)]

    near, far = CHUNKS
    held = len(near) * capacity
    (first, *first_codes), (second, *second_codes) = chosen
    came = swap_x(first)
    came_second = swap_x(second)
    sums = call(join_kernel, [shape(2, held, units)] * 4, [VMEM] * 2, moved=3 << 20)(*expand(came))
    came_second, _ = lax.optimization_barrier((came_second, sums))
    keep, got = expand(came_second)
    terms = spread(sums)
    mail = spread(
        call(turn_kernel, [shape(3, held, units)] * 4, [VMEM] * 6, moved=3 << 20)(*terms, keep, got)
    )
    parts = jnp.stack([m[2] for m in mail])
    others = along_section(parts, 0, 1)
    hidden = call(silu_kernel, shape(held, units), [VMEM] * 4, moved=1 << 20)(*mail)
    parts, hidden = lax.optimization_barrier((parts, hidden))
    pieces = spread([hidden] * 4)
    out, back = contract(parts, others)
    pieces, out = lax.optimization_barrier((pieces, out))
    parts = jnp.stack(pieces)
    others = along_section(parts, 0, 1)
    _, back_second = contract(parts, others)
    partials = mix(near, back, *first_codes) + mix(far, back_second, *second_codes)
    return sum(p.astype(F32) for p in partials).astype(BF16)


def solution(mesh):
    return jax.shard_map(
        body,
        mesh=mesh,
        in_specs=(
            P("expert", "section"),
            P("expert", None),
            P("expert", None),
            P("expert", "section", None),
            P("expert", "section", None),
            P("expert", None, "section"),
        ),
        out_specs=P("expert", "section"),
        check_vma=False,
    )
```

```python
import functools

import jax
import jax.numpy as jnp
from jax import lax
from jax.experimental import pallas as pl
from jax.experimental.pallas import tpu as pltpu
from jax.sharding import PartitionSpec as P

BF16, F32 = jnp.bfloat16, jnp.float32
NX, CORES = 4, 2
CHUNKS = ((1, -1, 2, -2), (0, 4, 3, -3))
VMEM = pl.BlockSpec(memory_space=pltpu.VMEM)
SMEM = pl.BlockSpec(memory_space=pltpu.SMEM)
HBM = pl.BlockSpec(memory_space=pltpu.HBM)


def along_expert(value, dz, dx):
    count = lax.axis_size("expert")
    planes = count // NX
    return lax.ppermute(
        value,
        "expert",
        [(i, (i // NX + dz) % planes * NX + (i % NX + dx) % NX) for i in range(count)],
    )


def along_section(value, dy, flip):
    count = lax.axis_size("section")
    return lax.ppermute(
        value, "section", [(i, (i + CORES * dy) % count ^ flip) for i in range(count)]
    )


def call(kernel, outs, specs=None, grid=(), out_specs=None, scratch=(), limit=20, flops=0, moved=0):
    return pl.pallas_call(
        kernel,
        grid=grid,
        out_shape=outs,
        in_specs=specs,
        out_specs=out_specs or jax.tree.map(lambda _: VMEM, outs),
        scratch_shapes=scratch,
        compiler_params=pltpu.CompilerParams(vmem_limit_bytes=limit << 20),
        cost_estimate=pl.CostEstimate(flops=16 * flops, bytes_accessed=16 * moved, transcendentals=0),
    )


def pack_kernel(rows, tokens_ref, routes_ref, combine_ref, out_ref, t_ref, r_ref, c_ref, sems):
    copies = [
        pltpu.make_async_copy(src, dst, sems.at[n])
        for n, (src, dst) in enumerate(
            ((tokens_ref, t_ref), (routes_ref, r_ref), (combine_ref, c_ref))
        )
    ]
    for copy in copies:
        copy.start()
    for copy in copies:
        copy.wait()
    out_ref[pl.ds(0, rows), :] = t_ref[...]
    info = jnp.concatenate([r_ref[...].astype(F32), c_ref[...]], axis=0)
    rest = jnp.zeros((info.shape[0], out_ref.shape[1] - rows), F32)
    out_ref[pl.ds(rows, 16), :] = jnp.concatenate([info, rest], axis=1).astype(BF16)


def select_kernel(capacity, rows, at_ref, *refs):
    nz = len(refs) - 3
    blocks, (out_ref, code_ref, weight_ref) = refs[:nz], refs[nz:]
    per_plane = 2 * NX
    row = lax.broadcasted_iota(jnp.int32, (per_plane, rows), 0)
    expert = (at_ref[0] * per_plane + row).astype(F32)
    earlier = (
        lax.broadcasted_iota(jnp.int32, (rows, rows), 0)
        < lax.broadcasted_iota(jnp.int32, (rows, rows), 1)
    ).astype(F32).astype(BF16)
    codes = []
    for n, block in enumerate(blocks):
        info = block[pl.ds(rows, 16), pl.ds(0, rows)].astype(F32)
        named = jnp.zeros((per_plane, rows), F32)
        weight = jnp.zeros((per_plane, rows), F32)
        for k in range(8):
            hit = info[k : k + 1] == expert
            named = named + jnp.where(hit, 1.0, 0.0)
            weight = weight + jnp.where(hit, info[8 + k : 9 + k], 0.0)
        slot = jnp.dot(named.astype(BF16), earlier, preferred_element_type=F32)
        codes.append(jnp.where(named > 0.5, slot + float(n * capacity), -1.0))
        weight_ref[:, pl.ds(n * rows, rows)] = weight
    code = jnp.concatenate(codes, axis=1)
    code_ref[...] = code
    held = nz * capacity
    at = lax.broadcasted_iota(jnp.int32, (held, nz * rows), 0).astype(F32)
    tokens = jnp.concatenate([block[pl.ds(0, rows), :] for block in blocks], axis=0)
    for r in range(NX):
        pick = jnp.concatenate(
            [jnp.where(at == code[2 * r + e : 2 * r + e + 1], 1.0, 0.0) for e in range(2)], axis=0
        ).astype(BF16)
        out_ref[r] = jnp.dot(pick, tokens, preferred_element_type=F32).astype(BF16)


def up_kernel(held, flip, at_ref, rows_ref, gate_ref, up_ref, out_ref, x_ref, w_ref, sems):
    y = at_ref[2]
    expert = (at_ref[1] + flip) % 2
    half = gate_ref.shape[2] // 2
    pieces = [(part, c) for c in range(2) for part in range(2)]

    def fetch(n):
        part, c = pieces[n]
        return pltpu.make_async_copy(
            (gate_ref, up_ref)[part].at[expert, :, pl.ds(c * half, half)], w_ref.at[n], sems.at[n]
        )

    fetch(0).start()
    fetch(1).start()
    for r in range(4):
        x_ref[pl.ds(r * held, held), :] = rows_ref[r, pl.ds(pl.multiple_of(expert * held, held), held), :]
    for n, (part, c) in enumerate(pieces):
        fetch(n).wait()
        if n < 2:
            fetch(n + 2).start()
        sums = jnp.dot(x_ref[...], w_ref[n], preferred_element_type=F32).astype(BF16)
        for r in range(4):
            out_ref[(r + 4 - y) % 4, part, :, pl.ds(c * half, half)] = sums[
                r * held : (r + 1) * held
            ]


def join_kernel(keep_ref, got_ref, *outs):
    for q in range(4):
        outs[q][...] = (keep_ref[q].astype(F32) + got_ref[q].astype(F32)).astype(BF16)


def activate(terms):
    gate, up = (
        (terms[0][i].astype(F32) + terms[1][i].astype(F32))
        + (terms[2][i].astype(F32) + terms[3][i].astype(F32))
        for i in range(2)
    )
    return (jax.nn.silu(gate) * up).astype(BF16)


def silu_kernel(*refs):
    refs[4][...] = activate(refs[:4])


def turn_kernel(*refs):
    terms, (keep_ref, got_ref), outs = refs[:4], refs[4:6], refs[6:]
    hidden = activate(terms)
    for q in range(4):
        outs[q][pl.ds(0, 2)] = (keep_ref[q].astype(F32) + got_ref[q].astype(F32)).astype(BF16)
        outs[q][2] = hidden


def down_kernel(held, at_ref, own_ref, other_ref, down_ref, *refs):
    apart = len(refs) == 7
    outs = refs[:4] if apart else [refs[0].at[d] for d in range(4)]
    h_ref, w_ref, sems = refs[-3:]
    core, y = at_ref[1], at_ref[2]
    x = at_ref[3] if apart else 0
    width = down_ref.shape[2]
    cuts = [pl.ds(0, 512), pl.ds(512, width - 512)]
    pieces = [(n, c) for n in range(2) for c in range(2)]

    def fetch(k):
        n, c = pieces[k]
        return pltpu.make_async_copy(
            down_ref.at[(core + n) % 2, :, cuts[c]], w_ref.at[n, :, cuts[c]], sems.at[k]
        )

    fetch(0).start()
    fetch(1).start()
    for n, parts_ref in enumerate((own_ref, other_ref)):
        for d in range(4):
            h_ref[n, pl.ds(d * held, held), :] = parts_ref[(y + 8 - x - d) % 4]
    for k, (n, c) in enumerate(pieces):
        fetch(k).wait()
        if k < 2:
            fetch(k + 2).start()
        got = jnp.dot(h_ref[n], w_ref[n, :, cuts[c]], preferred_element_type=F32).astype(BF16)
        for d in range(4):
            outs[d][(core + n) % 2, :, cuts[c]] = got[d * held : (d + 1) * held]


def mix_kernel(held, rows, apart, at_ref, *refs):
    backs, refs = (refs[:4], refs[4:]) if apart else ([refs[0].at[d] for d in range(4)], refs[1:])
    (code_ref, weight_ref), outs = refs[:2], refs[2:]
    width = code_ref.shape[1]
    at = lax.broadcasted_iota(jnp.int32, (held, width), 0).astype(F32)
    share = []
    for d in range(4):
        for e in range(2):
            j = pl.ds((at_ref[3] + 4 - d) % 4 * 2 + e, 1) if apart else pl.ds(2 * d + e, 1)
            share.append(jnp.where(at == code_ref[j, :], weight_ref[j, :], 0.0))
    back = jnp.concatenate([backs[d][e] for d in range(4) for e in range(2)], axis=0)
    total = lax.dot_general(
        jnp.concatenate(share, axis=0).astype(BF16),
        back,
        (((0,), (0,)), ((), ())),
        preferred_element_type=F32,
    ).astype(BF16)
    for n, out in enumerate(outs):
        out[...] = total[n * rows : (n + 1) * rows]


def shape(*dims, dtype=BF16):
    return jax.ShapeDtypeStruct(dims, dtype)


def body(tokens, routes, combine, gate_weight, up_weight, down_weight):
    groups = lax.axis_size("expert")
    per_device, width, units = gate_weight.shape
    rows, fanout = routes.shape
    capacity = 3 * rows * fanout // (2 * per_device * groups)
    place, part = lax.axis_index("expert"), lax.axis_index("section")
    at = jnp.stack([place // NX, part % CORES, part // CORES, place % NX]).astype(jnp.int32)
    planes = groups // NX
    x_groups = [[z * NX + x for x in range(NX)] for z in range(planes)]
    def swap_x(value):
        return lax.all_to_all(value, "expert", 0, 0, axis_index_groups=x_groups, tiled=True)

    gate_weight, up_weight, down_weight = (
        pltpu.with_memory_space_constraint(w, pltpu.HBM)
        for w in (gate_weight, up_weight, down_weight)
    )
    block = {
        0: call(
            functools.partial(pack_kernel, rows),
            shape(rows + 16, width),
            [HBM] * 3,
            scratch=[
                pltpu.VMEM((rows, width), BF16),
                pltpu.VMEM((fanout, rows), jnp.int32),
                pltpu.VMEM((fanout, rows), F32),
                pltpu.SemaphoreType.DMA((3,)),
            ],
            moved=1 << 19,
        )(*(pltpu.with_memory_space_constraint(v, pltpu.HBM) for v in (tokens, routes.T, combine.T)))
    }
    for d in (1, -1, 2, -2):
        step = 1 if d > 0 else -1
        block[d] = along_expert(block[d - step], step, 0)
    chosen = []
    for chunk in CHUNKS:
        nz = len(chunk)
        held = nz * capacity
        if chunk == CHUNKS[1]:
            own, ahead, behind, chosen = lax.optimization_barrier(
                (block[0], block[2], block[-2], chosen)
            )
            block[3], block[-3] = along_expert(ahead, 1, 0), along_expert(behind, -1, 0)
            block[4] = along_expert(own, 4, 0)
        chosen.append(
            call(
                functools.partial(select_kernel, capacity, rows),
                [shape(4, 2 * held, width)] + [shape(2 * NX, nz * rows, dtype=F32)] * 2,
                [SMEM] + [VMEM] * nz,
                flops=16 * held * nz * rows * width,
                moved=2 << 20,
            )(at, *[block[d] for d in chunk])
        )

    def expand(came):
        send, keep = (
            call(
                functools.partial(up_kernel, held, flip),
                shape(4, 2, held, units),
                [SMEM, VMEM, HBM, HBM],
                scratch=[
                    pltpu.VMEM((4 * held, width), BF16),
                    pltpu.VMEM((4, width, units // 2), BF16),
                    pltpu.SemaphoreType.DMA((4,)),
                ],
                flops=16 * held * width * units,
                moved=6 << 20,
            )(at, came, gate_weight, up_weight)
            for flip in (1, 0)
        )
        return keep, along_section(send, 0, 1)

    def spread(values):
        return [along_section(v, q, 0) if q else v for q, v in enumerate(values)]

    def contract(parts, others, apart):
        return call(
            functools.partial(down_kernel, held),
            [shape(2, held, width)] * 4 if apart else [shape(4, 2, held, width)],
            [SMEM, VMEM, VMEM, HBM],
            scratch=[
                pltpu.VMEM((2, 4 * held, units), BF16),
                pltpu.VMEM((2, units, width), BF16),
                pltpu.SemaphoreType.DMA((4,)),
            ],
            moved=1 << 10,
        )(at, parts, others, down_weight)

    def mix(chunk, back, code, weight):
        mixed = call(
            functools.partial(mix_kernel, held, rows, len(back) == 4),
            [shape(rows, width)] * len(chunk),
            [SMEM] + [VMEM] * (len(back) + 2),
            flops=16 * held * len(chunk) * rows * width,
            moved=2 << 20,
        )(at, *back, code, weight)
        return [along_expert(m, -d, 0) if d else m for d, m in zip(chunk, mixed)]

    near, far = CHUNKS
    held = len(near) * capacity
    (first, *first_codes), (second, *second_codes) = chosen
    came = swap_x(first)
    came_second = swap_x(second)
    sums = call(join_kernel, [shape(2, held, units)] * 4, [VMEM] * 2, moved=3 << 20)(*expand(came))
    came_second, _ = lax.optimization_barrier((came_second, sums))
    keep, got = expand(came_second)
    terms = spread(sums)
    mail = spread(
        call(turn_kernel, [shape(3, held, units)] * 4, [VMEM] * 6, moved=3 << 20)(*terms, keep, got)
    )
    parts = jnp.stack([m[2] for m in mail])
    others = along_section(parts, 0, 1)
    hidden = call(silu_kernel, shape(held, units), [VMEM] * 4, moved=1 << 20)(*mail)
    parts, hidden = lax.optimization_barrier((parts, hidden))
    pieces = spread([hidden] * 4)
    out = contract(parts, others, False)
    back = [swap_x(out[0])]
    pieces, out = lax.optimization_barrier((pieces, out))
    parts = jnp.stack(pieces)
    others = along_section(parts, 0, 1)
    out_second = contract(parts, others, True)
    back_second = [along_expert(v, 0, d) if d else v for d, v in enumerate(out_second)]
    partials = mix(near, back, *first_codes) + mix(far, back_second, *second_codes)
    return sum(p.astype(F32) for p in partials).astype(BF16)


def solution(mesh):
    return jax.shard_map(
        body,
        mesh=mesh,
        in_specs=(
            P("expert", "section"),
            P("expert", None),
            P("expert", None),
            P("expert", "section", None),
            P("expert", "section", None),
            P("expert", None, "section"),
        ),
        out_specs=P("expert", "section"),
        check_vma=False,
    )
```

```python
import functools

import jax
import jax.numpy as jnp
from jax import lax
from jax.experimental import pallas as pl
from jax.experimental.pallas import tpu as pltpu
from jax.sharding import PartitionSpec as P

BF16, F32 = jnp.bfloat16, jnp.float32
NX, CORES = 4, 2
CHUNKS = ((3, -3, 2, -2), (0, 4, 1, -1))
VMEM = pl.BlockSpec(memory_space=pltpu.VMEM)
SMEM = pl.BlockSpec(memory_space=pltpu.SMEM)
HBM = pl.BlockSpec(memory_space=pltpu.HBM)


def along_expert(value, dz, dx):
    count = lax.axis_size("expert")
    planes = count // NX
    return lax.ppermute(
        value,
        "expert",
        [(i, (i // NX + dz) % planes * NX + (i % NX + dx) % NX) for i in range(count)],
    )


def along_section(value, dy, flip):
    count = lax.axis_size("section")
    return lax.ppermute(
        value, "section", [(i, (i + CORES * dy) % count ^ flip) for i in range(count)]
    )


def call(kernel, outs, specs=None, grid=(), out_specs=None, scratch=(), limit=20, flops=0, moved=0):
    return pl.pallas_call(
        kernel,
        grid=grid,
        out_shape=outs,
        in_specs=specs,
        out_specs=out_specs or jax.tree.map(lambda _: VMEM, outs),
        scratch_shapes=scratch,
        compiler_params=pltpu.CompilerParams(vmem_limit_bytes=limit << 20),
        cost_estimate=pl.CostEstimate(flops=16 * flops, bytes_accessed=16 * moved, transcendentals=0),
    )


def pack_kernel(rows, tokens_ref, routes_ref, combine_ref, out_ref, t_ref, r_ref, c_ref, sems):
    copies = [
        pltpu.make_async_copy(src, dst, sems.at[n])
        for n, (src, dst) in enumerate(
            ((tokens_ref, t_ref), (routes_ref, r_ref), (combine_ref, c_ref))
        )
    ]
    for copy in copies:
        copy.start()
    for copy in copies:
        copy.wait()
    out_ref[pl.ds(0, rows), :] = t_ref[...]
    info = jnp.concatenate([r_ref[...].astype(F32), c_ref[...]], axis=0)
    rest = jnp.zeros((info.shape[0], out_ref.shape[1] - rows), F32)
    out_ref[pl.ds(rows, 16), :] = jnp.concatenate([info, rest], axis=1).astype(BF16)


def select_kernel(capacity, rows, at_ref, *refs):
    nz = len(refs) - 3
    blocks, (out_ref, code_ref, weight_ref) = refs[:nz], refs[nz:]
    per_plane = 2 * NX
    row = lax.broadcasted_iota(jnp.int32, (per_plane, rows), 0)
    expert = (at_ref[0] * per_plane + row).astype(F32)
    earlier = (
        lax.broadcasted_iota(jnp.int32, (rows, rows), 0)
        < lax.broadcasted_iota(jnp.int32, (rows, rows), 1)
    ).astype(F32).astype(BF16)
    codes = []
    for n, block in enumerate(blocks):
        info = block[pl.ds(rows, 16), pl.ds(0, rows)].astype(F32)
        named = jnp.zeros((per_plane, rows), F32)
        weight = jnp.zeros((per_plane, rows), F32)
        for k in range(8):
            hit = info[k : k + 1] == expert
            named = named + jnp.where(hit, 1.0, 0.0)
            weight = weight + jnp.where(hit, info[8 + k : 9 + k], 0.0)
        slot = jnp.dot(named.astype(BF16), earlier, preferred_element_type=F32)
        codes.append(jnp.where(named > 0.5, slot + float(n * capacity), -1.0))
        weight_ref[:, pl.ds(n * rows, rows)] = weight
    code = jnp.concatenate(codes, axis=1)
    code_ref[...] = code
    held = nz * capacity
    at = lax.broadcasted_iota(jnp.int32, (held, nz * rows), 0).astype(F32)
    tokens = jnp.concatenate([block[pl.ds(0, rows), :] for block in blocks], axis=0)
    for r in range(NX):
        pick = jnp.concatenate(
            [jnp.where(at == code[2 * r + e : 2 * r + e + 1], 1.0, 0.0) for e in range(2)], axis=0
        ).astype(BF16)
        out_ref[r] = jnp.dot(pick, tokens, preferred_element_type=F32).astype(BF16)


def up_kernel(held, flip, at_ref, rows_ref, gate_ref, up_ref, out_ref, x_ref, w_ref, sems):
    y = at_ref[2]
    expert = (at_ref[1] + flip) % 2
    half = gate_ref.shape[2] // 2
    pieces = [(part, c) for c in range(2) for part in range(2)]

    def fetch(n):
        part, c = pieces[n]
        return pltpu.make_async_copy(
            (gate_ref, up_ref)[part].at[expert, :, pl.ds(c * half, half)], w_ref.at[n], sems.at[n]
        )

    fetch(0).start()
    fetch(1).start()
    for r in range(4):
        x_ref[pl.ds(r * held, held), :] = rows_ref[r, pl.ds(pl.multiple_of(expert * held, held), held), :]
    for n, (part, c) in enumerate(pieces):
        fetch(n).wait()
        if n < 2:
            fetch(n + 2).start()
        sums = jnp.dot(x_ref[...], w_ref[n], preferred_element_type=F32).astype(BF16)
        for r in range(4):
            out_ref[(r + 4 - y) % 4, part, :, pl.ds(c * half, half)] = sums[
                r * held : (r + 1) * held
            ]


def join_kernel(keep_ref, got_ref, *outs):
    for q in range(4):
        outs[q][...] = (keep_ref[q].astype(F32) + got_ref[q].astype(F32)).astype(BF16)


def activate(terms):
    gate, up = (
        (terms[0][i].astype(F32) + terms[1][i].astype(F32))
        + (terms[2][i].astype(F32) + terms[3][i].astype(F32))
        for i in range(2)
    )
    return (jax.nn.silu(gate) * up).astype(BF16)


def silu_kernel(*refs):
    refs[4][...] = activate(refs[:4])


def turn_kernel(*refs):
    terms, (keep_ref, got_ref), outs = refs[:4], refs[4:6], refs[6:]
    hidden = activate(terms)
    for q in range(4):
        outs[q][pl.ds(0, 2)] = (keep_ref[q].astype(F32) + got_ref[q].astype(F32)).astype(BF16)
        outs[q][2] = hidden


def down_kernel(held, at_ref, own_ref, other_ref, down_ref, *refs):
    apart = len(refs) == 7
    outs = refs[:4] if apart else [refs[0].at[d] for d in range(4)]
    h_ref, w_ref, sems = refs[-3:]
    core, y = at_ref[1], at_ref[2]
    x = at_ref[3] if apart else 0
    width = down_ref.shape[2]
    cuts = [pl.ds(0, 512), pl.ds(512, width - 512)]
    pieces = [(n, c) for n in range(2) for c in range(2)]

    def fetch(k):
        n, c = pieces[k]
        return pltpu.make_async_copy(
            down_ref.at[(core + n) % 2, :, cuts[c]], w_ref.at[n, :, cuts[c]], sems.at[k]
        )

    fetch(0).start()
    fetch(1).start()
    for n, parts_ref in enumerate((own_ref, other_ref)):
        for d in range(4):
            h_ref[n, pl.ds(d * held, held), :] = parts_ref[(y + 8 - x - d) % 4]
    for k, (n, c) in enumerate(pieces):
        fetch(k).wait()
        if k < 2:
            fetch(k + 2).start()
        got = jnp.dot(h_ref[n], w_ref[n, :, cuts[c]], preferred_element_type=F32).astype(BF16)
        for d in range(4):
            outs[d][(core + n) % 2, :, cuts[c]] = got[d * held : (d + 1) * held]


def mix_kernel(held, rows, apart, at_ref, *refs):
    backs, refs = (refs[:4], refs[4:]) if apart else ([refs[0].at[d] for d in range(4)], refs[1:])
    (code_ref, weight_ref), outs = refs[:2], refs[2:]
    width = code_ref.shape[1]
    at = lax.broadcasted_iota(jnp.int32, (held, width), 0).astype(F32)
    share = []
    for d in range(4):
        for e in range(2):
            j = pl.ds((at_ref[3] + 4 - d) % 4 * 2 + e, 1) if apart else pl.ds(2 * d + e, 1)
            share.append(jnp.where(at == code_ref[j, :], weight_ref[j, :], 0.0))
    back = jnp.concatenate([backs[d][e] for d in range(4) for e in range(2)], axis=0)
    total = lax.dot_general(
        jnp.concatenate(share, axis=0).astype(BF16),
        back,
        (((0,), (0,)), ((), ())),
        preferred_element_type=F32,
    ).astype(BF16)
    for n, out in enumerate(outs):
        out[...] = total[n * rows : (n + 1) * rows]


def shape(*dims, dtype=BF16):
    return jax.ShapeDtypeStruct(dims, dtype)


def body(tokens, routes, combine, gate_weight, up_weight, down_weight):
    groups = lax.axis_size("expert")
    per_device, width, units = gate_weight.shape
    rows, fanout = routes.shape
    capacity = 3 * rows * fanout // (2 * per_device * groups)
    place, part = lax.axis_index("expert"), lax.axis_index("section")
    at = jnp.stack([place // NX, part % CORES, part // CORES, place % NX]).astype(jnp.int32)
    planes = groups // NX
    x_groups = [[z * NX + x for x in range(NX)] for z in range(planes)]
    def swap_x(value):
        return lax.all_to_all(value, "expert", 0, 0, axis_index_groups=x_groups, tiled=True)

    gate_weight, up_weight, down_weight = (
        pltpu.with_memory_space_constraint(w, pltpu.HBM)
        for w in (gate_weight, up_weight, down_weight)
    )
    block = {
        0: call(
            functools.partial(pack_kernel, rows),
            shape(rows + 16, width),
            [HBM] * 3,
            scratch=[
                pltpu.VMEM((rows, width), BF16),
                pltpu.VMEM((fanout, rows), jnp.int32),
                pltpu.VMEM((fanout, rows), F32),
                pltpu.SemaphoreType.DMA((3,)),
            ],
            moved=1 << 19,
        )(*(pltpu.with_memory_space_constraint(v, pltpu.HBM) for v in (tokens, routes.T, combine.T)))
    }
    for d in (1, -1, 2, -2, 3, -3):
        step = 1 if d > 0 else -1
        block[d] = along_expert(block[d - step], step, 0)
    chosen = []
    for chunk in CHUNKS:
        nz = len(chunk)
        held = nz * capacity
        if chunk == CHUNKS[1]:
            own, chosen = lax.optimization_barrier((block[0], chosen))
            block[4] = along_expert(own, 4, 0)
        chosen.append(
            call(
                functools.partial(select_kernel, capacity, rows),
                [shape(4, 2 * held, width)] + [shape(2 * NX, nz * rows, dtype=F32)] * 2,
                [SMEM] + [VMEM] * nz,
                flops=16 * held * nz * rows * width,
                moved=2 << 20,
            )(at, *[block[d] for d in chunk])
        )

    def expand(came):
        send, keep = (
            call(
                functools.partial(up_kernel, held, flip),
                shape(4, 2, held, units),
                [SMEM, VMEM, HBM, HBM],
                scratch=[
                    pltpu.VMEM((4 * held, width), BF16),
                    pltpu.VMEM((4, width, units // 2), BF16),
                    pltpu.SemaphoreType.DMA((4,)),
                ],
                flops=16 * held * width * units,
                moved=6 << 20,
            )(at, came, gate_weight, up_weight)
            for flip in (1, 0)
        )
        return keep, along_section(send, 0, 1)

    def spread(values):
        return [along_section(v, q, 0) if q else v for q, v in enumerate(values)]

    def contract(parts, others, apart):
        return call(
            functools.partial(down_kernel, held),
            [shape(2, held, width)] * 4 if apart else [shape(4, 2, held, width)],
            [SMEM, VMEM, VMEM, HBM],
            scratch=[
                pltpu.VMEM((2, 4 * held, units), BF16),
                pltpu.VMEM((2, units, width), BF16),
                pltpu.SemaphoreType.DMA((4,)),
            ],
            moved=1 << 10,
        )(at, parts, others, down_weight)

    def mix(chunk, back, code, weight):
        return call(
            functools.partial(mix_kernel, held, rows, len(back) == 4),
            [shape(rows, width)] * len(chunk),
            [SMEM] + [VMEM] * (len(back) + 2),
            flops=16 * held * len(chunk) * rows * width,
            moved=2 << 20,
        )(at, *back, code, weight)

    def add(*values):
        return sum(v.astype(F32) for v in values).astype(BF16)

    far, near = CHUNKS
    held = len(far) * capacity
    (first, *first_codes), (second, *second_codes) = chosen
    came = swap_x(first)
    came_second = swap_x(second)
    sums = call(join_kernel, [shape(2, held, units)] * 4, [VMEM] * 2, moved=3 << 20)(*expand(came))
    came_second, _ = lax.optimization_barrier((came_second, sums))
    keep, got = expand(came_second)
    terms = spread(sums)
    mail = spread(
        call(turn_kernel, [shape(3, held, units)] * 4, [VMEM] * 6, moved=3 << 20)(*terms, keep, got)
    )
    parts = jnp.stack([m[2] for m in mail])
    others = along_section(parts, 0, 1)
    hidden = call(silu_kernel, shape(held, units), [VMEM] * 4, moved=1 << 20)(*mail)
    parts, hidden = lax.optimization_barrier((parts, hidden))
    pieces = spread([hidden] * 4)
    out = contract(parts, others, False)
    back = [swap_x(out[0])]
    pieces, out = lax.optimization_barrier((pieces, out))
    parts = jnp.stack(pieces)
    others = along_section(parts, 0, 1)
    out_second = contract(parts, others, True)
    back_second = [along_expert(v, 0, d) if d else v for d, v in enumerate(out_second)]
    up_3, down_3, up_2, down_2 = mix(far, back, *first_codes)
    own, across, up_1, down_1 = mix(near, back_second, *second_codes)
    up_2 = add(up_2, along_expert(up_3, -1, 0))
    down_2 = add(down_2, along_expert(down_3, 1, 0))
    up_1 = add(up_1, along_expert(up_2, -1, 0))
    down_1 = add(down_1, along_expert(down_2, 1, 0))
    return add(
        own, along_expert(across, -4, 0), along_expert(up_1, -1, 0), along_expert(down_1, 1, 0)
    )


def solution(mesh):
    return jax.shard_map(
        body,
        mesh=mesh,
        in_specs=(
            P("expert", "section"),
            P("expert", None),
            P("expert", None),
            P("expert", "section", None),
            P("expert", "section", None),
            P("expert", None, "section"),
        ),
        out_specs=P("expert", "section"),
        check_vma=False,
    )
```

```python
import functools

import jax
import jax.numpy as jnp
from jax import lax
from jax.experimental import pallas as pl
from jax.experimental.pallas import tpu as pltpu
from jax.sharding import PartitionSpec as P

BF16, F32 = jnp.bfloat16, jnp.float32
NX, CORES = 4, 2
CHUNKS = ((3, -3, 2, -2), (0, 4, 1, -1))
VMEM = pl.BlockSpec(memory_space=pltpu.VMEM)
SMEM = pl.BlockSpec(memory_space=pltpu.SMEM)
HBM = pl.BlockSpec(memory_space=pltpu.HBM)


def along_expert(value, dz, dx):
    count = lax.axis_size("expert")
    planes = count // NX
    return lax.ppermute(
        value,
        "expert",
        [(i, (i // NX + dz) % planes * NX + (i % NX + dx) % NX) for i in range(count)],
    )


def along_section(value, dy, flip):
    count = lax.axis_size("section")
    return lax.ppermute(
        value, "section", [(i, (i + CORES * dy) % count ^ flip) for i in range(count)]
    )


def call(kernel, outs, specs=None, grid=(), out_specs=None, scratch=(), limit=20, flops=0, moved=0):
    return pl.pallas_call(
        kernel,
        grid=grid,
        out_shape=outs,
        in_specs=specs,
        out_specs=out_specs or jax.tree.map(lambda _: VMEM, outs),
        scratch_shapes=scratch,
        compiler_params=pltpu.CompilerParams(vmem_limit_bytes=limit << 20),
        cost_estimate=pl.CostEstimate(flops=16 * flops, bytes_accessed=16 * moved, transcendentals=0),
    )


def pack_kernel(rows, tokens_ref, routes_ref, combine_ref, out_ref, t_ref, r_ref, c_ref, sems):
    copies = [
        pltpu.make_async_copy(src, dst, sems.at[n])
        for n, (src, dst) in enumerate(
            ((tokens_ref, t_ref), (routes_ref, r_ref), (combine_ref, c_ref))
        )
    ]
    for copy in copies:
        copy.start()
    for copy in copies:
        copy.wait()
    out_ref[pl.ds(0, rows), :] = t_ref[...]
    info = jnp.concatenate([r_ref[...].astype(F32), c_ref[...]], axis=0)
    rest = jnp.zeros((info.shape[0], out_ref.shape[1] - rows), F32)
    out_ref[pl.ds(rows, 16), :] = jnp.concatenate([info, rest], axis=1).astype(BF16)


def select_kernel(capacity, rows, at_ref, *refs):
    nz = len(refs) - 3
    blocks, (out_ref, code_ref, weight_ref) = refs[:nz], refs[nz:]
    per_plane = 2 * NX
    row = lax.broadcasted_iota(jnp.int32, (per_plane, rows), 0)
    expert = (at_ref[0] * per_plane + row).astype(F32)
    earlier = (
        lax.broadcasted_iota(jnp.int32, (rows, rows), 0)
        < lax.broadcasted_iota(jnp.int32, (rows, rows), 1)
    ).astype(F32).astype(BF16)
    codes = []
    for n, block in enumerate(blocks):
        info = block[pl.ds(rows, 16), pl.ds(0, rows)].astype(F32)
        named = jnp.zeros((per_plane, rows), F32)
        weight = jnp.zeros((per_plane, rows), F32)
        for k in range(8):
            hit = info[k : k + 1] == expert
            named = named + jnp.where(hit, 1.0, 0.0)
            weight = weight + jnp.where(hit, info[8 + k : 9 + k], 0.0)
        slot = jnp.dot(named.astype(BF16), earlier, preferred_element_type=F32)
        codes.append(jnp.where(named > 0.5, slot + float(n * capacity), -1.0))
        weight_ref[:, pl.ds(n * rows, rows)] = weight
    code = jnp.concatenate(codes, axis=1)
    code_ref[...] = code
    held = nz * capacity
    at = lax.broadcasted_iota(jnp.int32, (held, nz * rows), 0).astype(F32)
    tokens = jnp.concatenate([block[pl.ds(0, rows), :] for block in blocks], axis=0)
    for r in range(NX):
        pick = jnp.concatenate(
            [jnp.where(at == code[2 * r + e : 2 * r + e + 1], 1.0, 0.0) for e in range(2)], axis=0
        ).astype(BF16)
        out_ref[r] = jnp.dot(pick, tokens, preferred_element_type=F32).astype(BF16)


def up_kernel(held, flip, at_ref, rows_ref, gate_ref, up_ref, out_ref, x_ref, w_ref, sems):
    y = at_ref[2]
    expert = (at_ref[1] + flip) % 2
    half = gate_ref.shape[2] // 2
    pieces = [(part, c) for c in range(2) for part in range(2)]

    def fetch(n):
        part, c = pieces[n]
        return pltpu.make_async_copy(
            (gate_ref, up_ref)[part].at[expert, :, pl.ds(c * half, half)], w_ref.at[n], sems.at[n]
        )

    fetch(0).start()
    fetch(1).start()
    for r in range(4):
        x_ref[pl.ds(r * held, held), :] = rows_ref[r, pl.ds(pl.multiple_of(expert * held, held), held), :]
    for n, (part, c) in enumerate(pieces):
        fetch(n).wait()
        if n < 2:
            fetch(n + 2).start()
        sums = jnp.dot(x_ref[...], w_ref[n], preferred_element_type=F32).astype(BF16)
        for r in range(4):
            out_ref[(r + 4 - y) % 4, part, :, pl.ds(c * half, half)] = sums[
                r * held : (r + 1) * held
            ]


def join_kernel(keep_ref, got_ref, *outs):
    for q in range(4):
        outs[q][...] = (keep_ref[q].astype(F32) + got_ref[q].astype(F32)).astype(BF16)


def activate(terms):
    gate, up = (
        (terms[0][i].astype(F32) + terms[1][i].astype(F32))
        + (terms[2][i].astype(F32) + terms[3][i].astype(F32))
        for i in range(2)
    )
    return (jax.nn.silu(gate) * up).astype(BF16)


def silu_kernel(*refs):
    refs[4][...] = activate(refs[:4])


def turn_kernel(*refs):
    terms, (keep_ref, got_ref), outs = refs[:4], refs[4:6], refs[6:]
    hidden = activate(terms)
    for q in range(4):
        outs[q][pl.ds(0, 2)] = (keep_ref[q].astype(F32) + got_ref[q].astype(F32)).astype(BF16)
        outs[q][2] = hidden


def down_kernel(held, at_ref, own_ref, other_ref, down_ref, *refs):
    apart = len(refs) == 7
    outs = refs[:4] if apart else [refs[0].at[d] for d in range(4)]
    h_ref, w_ref, sems = refs[-3:]
    core, y = at_ref[1], at_ref[2]
    x = at_ref[3] if apart else 0
    width = down_ref.shape[2]
    cuts = [pl.ds(0, 512), pl.ds(512, width - 512)]
    pieces = [(n, c) for n in range(2) for c in range(2)]

    def fetch(k):
        n, c = pieces[k]
        return pltpu.make_async_copy(
            down_ref.at[(core + n) % 2, :, cuts[c]], w_ref.at[n, :, cuts[c]], sems.at[k]
        )

    fetch(0).start()
    fetch(1).start()
    for n, parts_ref in enumerate((own_ref, other_ref)):
        for d in range(4):
            h_ref[n, pl.ds(d * held, held), :] = parts_ref[(y + 8 - x - d) % 4]
    for k, (n, c) in enumerate(pieces):
        fetch(k).wait()
        if k < 2:
            fetch(k + 2).start()
        got = jnp.dot(h_ref[n], w_ref[n, :, cuts[c]], preferred_element_type=F32).astype(BF16)
        for d in range(4):
            outs[d][(core + n) % 2, :, cuts[c]] = got[d * held : (d + 1) * held]


def mix_kernel(held, rows, apart, at_ref, *refs):
    backs, refs = (refs[:4], refs[4:]) if apart else ([refs[0].at[d] for d in range(4)], refs[1:])
    (code_ref, weight_ref), outs = refs[:2], refs[2:]
    width = code_ref.shape[1]
    at = lax.broadcasted_iota(jnp.int32, (held, width), 0).astype(F32)
    share = []
    for d in range(4):
        for e in range(2):
            j = pl.ds((at_ref[3] + 4 - d) % 4 * 2 + e, 1) if apart else pl.ds(2 * d + e, 1)
            share.append(jnp.where(at == code_ref[j, :], weight_ref[j, :], 0.0))
    back = jnp.concatenate([backs[d][e] for d in range(4) for e in range(2)], axis=0)
    total = lax.dot_general(
        jnp.concatenate(share, axis=0).astype(BF16),
        back,
        (((0,), (0,)), ((), ())),
        preferred_element_type=F32,
    ).astype(BF16)
    for n, out in enumerate(outs):
        out[...] = total[n * rows : (n + 1) * rows]


def shape(*dims, dtype=BF16):
    return jax.ShapeDtypeStruct(dims, dtype)


def body(tokens, routes, combine, gate_weight, up_weight, down_weight):
    groups = lax.axis_size("expert")
    per_device, width, units = gate_weight.shape
    rows, fanout = routes.shape
    capacity = 3 * rows * fanout // (2 * per_device * groups)
    place, part = lax.axis_index("expert"), lax.axis_index("section")
    at = jnp.stack([place // NX, part % CORES, part // CORES, place % NX]).astype(jnp.int32)
    planes = groups // NX
    x_groups = [[z * NX + x for x in range(NX)] for z in range(planes)]
    def swap_x(value):
        return lax.all_to_all(value, "expert", 0, 0, axis_index_groups=x_groups, tiled=True)

    gate_weight, up_weight, down_weight = (
        pltpu.with_memory_space_constraint(w, pltpu.HBM)
        for w in (gate_weight, up_weight, down_weight)
    )
    block = {
        0: call(
            functools.partial(pack_kernel, rows),
            shape(rows + 16, width),
            [HBM] * 3,
            scratch=[
                pltpu.VMEM((rows, width), BF16),
                pltpu.VMEM((fanout, rows), jnp.int32),
                pltpu.VMEM((fanout, rows), F32),
                pltpu.SemaphoreType.DMA((3,)),
            ],
            moved=1 << 19,
        )(*(pltpu.with_memory_space_constraint(v, pltpu.HBM) for v in (tokens, routes.T, combine.T)))
    }
    for d in (1, -1, 2, -2, 3, -3):
        step = 1 if d > 0 else -1
        block[d] = along_expert(block[d - step], step, 0)
    chosen = []
    for chunk in CHUNKS:
        nz = len(chunk)
        held = nz * capacity
        if chunk == CHUNKS[1]:
            own, chosen = lax.optimization_barrier((block[0], chosen))
            block[4] = along_expert(own, 4, 0)
        chosen.append(
            call(
                functools.partial(select_kernel, capacity, rows),
                [shape(4, 2 * held, width)] + [shape(2 * NX, nz * rows, dtype=F32)] * 2,
                [SMEM] + [VMEM] * nz,
                flops=16 * held * nz * rows * width,
                moved=2 << 20,
            )(at, *[block[d] for d in chunk])
        )

    def expand(came):
        send, keep = (
            call(
                functools.partial(up_kernel, held, flip),
                shape(4, 2, held, units),
                [SMEM, VMEM, HBM, HBM],
                scratch=[
                    pltpu.VMEM((4 * held, width), BF16),
                    pltpu.VMEM((4, width, units // 2), BF16),
                    pltpu.SemaphoreType.DMA((4,)),
                ],
                flops=16 * held * width * units,
                moved=6 << 20,
            )(at, came, gate_weight, up_weight)
            for flip in (1, 0)
        )
        return keep, along_section(send, 0, 1)

    def spread(values):
        return [along_section(v, q, 0) if q else v for q, v in enumerate(values)]

    def contract(parts, others, apart):
        return call(
            functools.partial(down_kernel, held),
            [shape(2, held, width)] * 4 if apart else [shape(4, 2, held, width)],
            [SMEM, VMEM, VMEM, HBM],
            scratch=[
                pltpu.VMEM((2, 4 * held, units), BF16),
                pltpu.VMEM((2, units, width), BF16),
                pltpu.SemaphoreType.DMA((4,)),
            ],
            moved=1 << 10,
        )(at, parts, others, down_weight)

    def mix(chunk, back, code, weight):
        return call(
            functools.partial(mix_kernel, held, rows, len(back) == 4),
            [shape(rows, width)] * len(chunk),
            [SMEM] + [VMEM] * (len(back) + 2),
            flops=16 * held * len(chunk) * rows * width,
            moved=2 << 20,
        )(at, *back, code, weight)

    def add(*values):
        return sum(v.astype(F32) for v in values).astype(BF16)

    far, near = CHUNKS
    held = len(far) * capacity
    (first, *first_codes), (second, *second_codes) = chosen
    came = swap_x(first)
    came_second = swap_x(second)
    sums = call(join_kernel, [shape(2, held, units)] * 4, [VMEM] * 2, moved=3 << 20)(*expand(came))
    came_second, _ = lax.optimization_barrier((came_second, sums))
    keep, got = expand(came_second)
    terms = spread(sums)
    mail = spread(
        call(turn_kernel, [shape(3, held, units)] * 4, [VMEM] * 6, moved=3 << 20)(*terms, keep, got)
    )
    parts = jnp.stack([m[2] for m in mail])
    others = along_section(parts, 0, 1)
    hidden = call(silu_kernel, shape(held, units), [VMEM] * 4, moved=1 << 20)(*mail)
    parts, hidden = lax.optimization_barrier((parts, hidden))
    pieces = spread([hidden] * 4)
    out = contract(parts, others, False)
    back = [swap_x(out[0])]
    pieces, out = lax.optimization_barrier((pieces, out))
    parts = jnp.stack(pieces)
    others = along_section(parts, 0, 1)
    out_second = contract(parts, others, True)
    back_second = [along_expert(v, 0, d) if d else v for d, v in enumerate(out_second)]
    up_3, down_3, up_2, down_2 = mix(far, back, *first_codes)
    up_2 = add(up_2, along_expert(up_3, -1, 0))
    down_2 = add(down_2, along_expert(down_3, 1, 0))
    back_second, _ = lax.optimization_barrier((back_second, (up_2, down_2)))
    own, across, up_1, down_1 = mix(near, back_second, *second_codes)
    up_1 = add(up_1, along_expert(up_2, -1, 0))
    down_1 = add(down_1, along_expert(down_2, 1, 0))
    return add(
        own, along_expert(across, -4, 0), along_expert(up_1, -1, 0), along_expert(down_1, 1, 0)
    )


def solution(mesh):
    return jax.shard_map(
        body,
        mesh=mesh,
        in_specs=(
            P("expert", "section"),
            P("expert", None),
            P("expert", None),
            P("expert", "section", None),
            P("expert", "section", None),
            P("expert", None, "section"),
        ),
        out_specs=P("expert", "section"),
        check_vma=False,
    )
```
